256 devices in a mesh: fsdp: 64 (over x, z, core), rep: 4 (over y).
Axes of the slice: x: 4, y: 4, z: 8, core: 2. Of those that a mesh axis runs over, the one named last changes fastest.
Arguments:
- grads: bfloat16 [2, 16, 512, 6144], P(None, None, 'fsdp', 'rep'), may hold values from -8 to 8
- second_moment: float32 [2, 16, 512, 6144], P(None, None, 'fsdp', 'rep'), may hold values from 0.015 to 10, as said below
- momentum: float32 [2, 16, 512, 6144], P(None, None, 'fsdp', 'rep'), may hold values from -6 to 6
- left_inverse_root: float32 [4, 64, 3, 512, 512], P('rep', 'fsdp'), may hold values from -1 to 6, as said below
- right_root: float32 [4, 64, 3, 512, 512], P('rep', 'fsdp'), may hold values from -1 to 6, as said below
- owner: int32 [4, 96], P('rep'), may hold values from 0 to 63, as said below
- slot: int32 [4, 96], P('rep'), may hold values from 0 to 2, as said below
Outputs:
- moment_new: float32 [2, 16, 512, 6144], P(None, None, 'fsdp', 'rep')
- momentum_new: float32 [2, 16, 512, 6144], P(None, None, 'fsdp', 'rep')
The draws below stay inside these ranges and needn't reach their ends.
Inputs may be any that keep to these rules, and one draw needn't show every extreme that they name: Within one rep index no two blocks share an (owner, slot) pair, and some owner holds 3 blocks. `slot`: slots of the blocks at their owners, as described for owner. `left_inverse_root`: symmetric factors. `right_root`: symmetric factors. `second_moment`: positive second moments.
All inputs are finite; a program needn't handle non-finite values.
Results may differ from the reference program's by a relative error of at most 0.0003.
Values may be sent and summed in bfloat16 or wider, within the bound.
A program may use at most 64 MiB of HBM per device.

```python
import math
import jax
import jax.numpy as jnp
from jax import lax

B = 512
ROWBLK = 16
COLS = 6144
NBR = 96
SLOTS = 3
N_FSDP = 64
N_REP = 4


def assignment(key):

    def group(group_key):
        key_order, key_heavy, key_blocks = jax.random.split(group_key, 3)
        total = N_FSDP * SLOTS
        heavy = jax.random.randint(key_heavy, (), 0, N_FSDP)
        order = jax.random.permutation(key_order, total).astype(jnp.int32)
        score = jnp.where(order // SLOTS == heavy, 0, 1).astype(jnp.int32)
        first = order[jnp.argsort(score, stable=True)][:NBR]
        blocks = jax.random.permutation(key_blocks, NBR)
        return jnp.zeros((NBR,), jnp.int32).at[blocks].set(first)
    keys = jax.vmap(lambda index: jax.random.fold_in(key, index))(jnp.arange(N_REP))
    return jax.vmap(group)(keys)


def factor(key):
    key_diag, key_off = jax.random.split(key)
    block_shape = (N_REP, N_FSDP, SLOTS, B)
    diag = jnp.exp(jax.random.uniform(key_diag, block_shape, jnp.float32, math.log(0.6), math.log(3.0)))
    spread = 2.0 / math.sqrt(B)
    common = 2.5 / B
    noise = jax.random.uniform(key_off, block_shape + (B,), jnp.float32, -spread, spread)
    symmetric = 0.5 * (noise + jnp.swapaxes(noise, -1, -2))
    rows = jnp.arange(B)[:, None]
    cols = jnp.arange(B)[None, :]
    on_diag = (rows == cols).astype(jnp.float32)
    return symmetric * (1.0 - on_diag) + on_diag * diag[..., None] + common


def draw_owner(key, part):
    return (assignment(key) // SLOTS).astype(jnp.int32)


def draw_slot(key, part):
    return (assignment(key) % SLOTS).astype(jnp.int32)


def draw_left_inverse_root(key, part):
    key = jax.random.fold_in(key, 11)
    return factor(key)


def draw_right_root(key, part):
    key = jax.random.fold_in(key, 12)
    return factor(key)


def draw_second_moment(key, part):
    key = jax.random.fold_in(key, 13)
    block_shape = (2, ROWBLK, B, COLS)
    within = jnp.arange(B, dtype=jnp.float32)[None, None, :, None] / (B - 1)
    across = jnp.arange(COLS, dtype=jnp.float32)[None, None, None, :] / (COLS - 1)
    noise = jnp.exp(jax.random.uniform(key, block_shape, jnp.float32, -1.2, 1.2))
    return noise * jnp.power(3.0, -within - across)


def draw_grads(key, part):
    key = jax.random.fold_in(key, 14)
    key_sign, key_rows, key_cols, key_noise = jax.random.split(key, 4)
    sign = (2 * jax.random.randint(key_sign, (2, ROWBLK, 1, 1), 0, 2) - 1).astype(jnp.float32)
    row_part = jnp.exp(jax.random.uniform(key_rows, (2, ROWBLK, B, 1), jnp.float32, math.log(0.5), math.log(2.0)))
    col_part = jnp.clip(jax.random.normal(key_cols, (2, ROWBLK, 1, COLS), jnp.float32), -3.0, 3.0)
    noise = 0.6 * jnp.clip(jax.random.normal(key_noise, (2, ROWBLK, B, COLS), jnp.float32), -4.0, 4.0)
    value = 0.8 * sign * row_part * col_part + noise
    return jnp.clip(value, -8.0, 8.0).astype(jnp.bfloat16)


def steps_of(stream_key, dims, shards, least, top_value):
    factor_of = 1.0
    for position, blocks in shards:
        heights = jax.random.uniform(jax.random.fold_in(jax.random.fold_in(stream_key, 6), position), (blocks,), jnp.float32, least / len(shards), top_value / len(shards))
        factor_of = factor_of * jnp.repeat(jnp.exp(heights), dims[position] // blocks).reshape((-1,) + (1,) * (len(dims) - 1 - position))
    return factor_of


def normal_values(rng, dims, scale, bound, cuts=(), kind=jnp.bfloat16):
    entries = scale * jax.random.normal(rng, dims, jnp.float32)
    if cuts:
        entries = entries * steps_of(rng, dims, cuts, -0.22, 0.18)
    return jnp.clip(entries, -bound, bound).astype(kind)


def setup_inputs(seed: int = 0) -> dict:
    key_of = jax.random.split(jax.random.key(seed), 8)
    grads = draw_grads(jax.random.fold_in(key_of[7], 71), 0)
    second_moment = draw_second_moment(jax.random.fold_in(key_of[7], 71), 0)
    momentum = normal_values(key_of[2], (2, ROWBLK, B, COLS), 1.0, 6.0, ((2, 64), (3, 4)), jnp.float32)
    left_inverse_root = draw_left_inverse_root(jax.random.fold_in(key_of[7], 71), 0)
    right_root = draw_right_root(jax.random.fold_in(key_of[7], 71), 0)
    owner = draw_owner(jax.random.fold_in(key_of[7], 71), 0)
    slot = draw_slot(jax.random.fold_in(key_of[7], 71), 0)
    return dict(grads=grads, second_moment=second_moment, momentum=momentum, left_inverse_root=left_inverse_root, right_root=right_root, owner=owner, slot=slot)


def precondition(g_full, left_inverse_root, right_root, owner, slot):
    nrep = left_inverse_root.shape[0]
    block_item = left_inverse_root.shape[-1]
    two, rowblk, inner, cols = g_full.shape
    colblk = cols // (nrep * block_item)
    nblocks = two * rowblk * colblk
    tile_blocks = g_full.reshape(two, rowblk, block_item, nrep, colblk, block_item).transpose(3, 0, 1, 4, 2, 5)
    tile_blocks = tile_blocks.reshape(nrep * nblocks, block_item, block_item)
    rep_of = (jnp.arange(nrep * nblocks) // nblocks).astype(jnp.int32)
    owners = owner.reshape(-1).astype(jnp.int32)
    slots = slot.reshape(-1).astype(jnp.int32)

    def single(items):
        tile, rep_index, own, place = items
        left = left_inverse_root[rep_index, own, place]
        right = right_root[rep_index, own, place]
        inner_prod = jnp.dot(tile, right, precision=lax.Precision.HIGHEST)
        return jnp.dot(left, inner_prod, precision=lax.Precision.HIGHEST)
    result = lax.map(single, (tile_blocks, rep_of, owners, slots))
    result = result.reshape(nrep, two, rowblk, colblk, block_item, block_item).transpose(1, 2, 4, 0, 3, 5)
    return result.reshape(two, rowblk, block_item, cols)

def reference(grads, second_moment, momentum, left_inverse_root, right_root, owner, slot):
    g_full = grads.astype(jnp.float32)
    moment_new = 0.9 * second_moment + 0.1 * g_full * g_full
    adam = g_full / (jnp.sqrt(moment_new) + 1e-08)
    adam_sq = lax.optimization_barrier(jnp.sum(adam * adam, axis=(1, 2, 3)))
    direction = precondition(g_full, left_inverse_root, right_root, owner, slot)
    shampoo_sq = lax.optimization_barrier(jnp.sum(direction * direction, axis=(1, 2, 3)))
    scale = jnp.sqrt(adam_sq) / (jnp.sqrt(shampoo_sq) + 1e-06)
    momentum_new = 0.9 * momentum + scale[:, None, None, None] * direction
    return (moment_new, momentum_new)
```

```python
import functools

import jax
import jax.numpy as jnp
from jax import lax
from jax.experimental import pallas as pl
from jax.experimental.pallas import tpu as pltpu
from jax.sharding import PartitionSpec as P

MESH = pl.DeviceIdType.MESH
NX, NZ, NC, NREP = 4, 8, 2, 4
LINE = NX * NC
SLOTS = 3
B = 512
NBLK = 96
PLACES = LINE * SLOTS
CAP = 24
STEPS = 16.0


def offset_of(k):
    return jnp.where(k % 2 == 1, (k + 1) // 2, (NZ - k // 2) % NZ)


def tables(owner, slot, cap):
    f = lax.axis_index("fsdp")
    x, z, c = f // (NZ * NC), (f // NC) % NZ, f % NC
    blocks = jnp.arange(NBLK, dtype=jnp.int32)
    line = (owner // NC) % NZ
    ox, oc = owner // (NZ * NC), owner % NC
    place = (ox * NC + oc) * SLOTS + slot
    before = (line[None, :] == line[:, None]) & (place[None, :] < place[:, None])
    rank = jnp.sum(before.astype(jnp.int32), axis=1)

    def pick(key, wanted, value):
        return jnp.sum(jnp.where(wanted[:, None] == key[None, :], value[None, :], 0), axis=1)

    line_pos = line * 32 + rank
    dist = jnp.arange(NZ, dtype=jnp.int32)
    pos = jnp.arange(cap, dtype=jnp.int32)
    wanted = (((z + dist) % NZ) * 32)[:, None] + pos[None, :]
    outgoing = pick(line_pos, wanted.reshape(-1), blocks)
    here = line * 32 + place
    j = jnp.arange(LINE, dtype=jnp.int32)
    jx, jc = (x + j // NC) % NX, (c + j % NC) % NC
    jplace = ((jx * NC + jc) * SLOTS)[:, None] + jnp.arange(SLOTS, dtype=jnp.int32)[None, :]
    deal = jnp.minimum(pick(here, z * 32 + jplace.reshape(-1), rank), cap - 1)
    code = (((x - ox) % NX) * NC + (oc + c) % NC) * SLOTS + slot
    collect = pick(line_pos, z * 32 + pos, code)
    mine = pick(here, z * 32 + (x * NC + c) * SLOTS + jnp.arange(SLOTS, dtype=jnp.int32), 1 + blocks // (NBLK // 2))
    over = jnp.max(rank) >= cap
    parts = [outgoing, deal, collect, mine, over.astype(jnp.int32)[None], (z - line) % NZ, jnp.minimum(rank, cap - 1), place]
    offs, at = [], 0
    for part in parts:
        offs.append(at)
        at += part.shape[0]
    return jnp.concatenate(parts).astype(jnp.int32), offs


def kernel(cap, offs, np_groups, tab, g_ref, sm_hbm, mom_hbm, left_hbm, right_hbm,
           mn_hbm, out_hbm, stat_ref,
           gp, sm, mom, mn, lf, rf, lhi, llo, rhi, rlo, thi, tlo, pbuf,
           zout, zin, xout, xin, xrout, xrin, zrout, zrin, zst, xst, nrm, nin, tot,
           lsem, osem, zs, zr, xs, xr, xrs, xrr, zrs, zrr, ns, nr):
    o_out, o_deal, o_col, o_mine, o_over, o_fd, o_fp, o_fe = offs
    f = lax.axis_index("fsdp")
    r = lax.axis_index("rep")
    x, z, c = f // (NZ * NC), (f // NC) % NZ, f % NC
    f32 = jnp.float32

    def zdev(d):
        return (x * (NZ * NC) + lax.rem(z + d, NZ) * NC + c, r)

    def xdev(j):
        return (lax.rem(x + j // NC, NX) * (NZ * NC) + z * NC + lax.rem(c + j % NC, NC), r)

    def rdev(i):
        return (f, lax.rem(r + i, NREP))

    peers = [zdev(d) for d in range(1, NZ)] + [xdev(j) for j in range(1, LINE)] + [rdev(i) for i in range(1, NREP)]
    bar = pltpu.get_barrier_semaphore()
    for dev in peers:
        pl.semaphore_signal(bar, 1, device_id=dev, device_id_type=MESH)

    loads = [
        pltpu.make_async_copy(right_hbm, rf, lsem.at[0]),
        pltpu.make_async_copy(sm_hbm, sm, lsem.at[1]),
        pltpu.make_async_copy(left_hbm, lf, lsem.at[2]),
        pltpu.make_async_copy(mom_hbm, mom, lsem.at[3]),
    ]
    for cp in loads:
        cp.start()

    def repack(i, carry):
        row = g_ref[i].astype(f32)
        for q in range(3):
            a = row[:, q * B:q * B + B // 2]
            b = row[:, q * B + B // 2:(q + 1) * B]
            gp[i * 3 + q] = jnp.concatenate([a, b], axis=0).astype(jnp.bfloat16)
        return carry

    lax.fori_loop(0, 32, repack, 0)

    def fill(d, dst, slot):
        def one(p, carry):
            dst[slot, p] = gp[tab[o_out + d * cap + p]]
            return carry
        lax.fori_loop(0, cap, one, 0, unroll=6)

    def zsend(k, carry):
        d = offset_of(k)
        fill(d, zout, d)

        @pl.when(k == 1)
        def _():
            pl.semaphore_wait(bar, len(peers))

        pltpu.make_async_remote_copy(src_ref=zout.at[d], dst_ref=zin.at[d], send_sem=zs, recv_sem=zr.at[d],
                                     device_id=zdev(d), device_id_type=MESH).start()
        return carry

    lax.fori_loop(1, NZ, zsend, 0)
    fill(0, zin, 0)

    loads[1].wait()

    def adam_m(m):
        def one(k, acc):
            i = m * 16 + k
            g = g_ref[i].astype(f32)
            new = 0.9 * sm[i] + 0.1 * g * g
            mn[i] = new
            a = g / (jnp.sqrt(new) + 1e-8)
            a = a * a
            for q in range(12):
                acc = acc + a[:, q * 128:(q + 1) * 128]
            return acc
        return lax.fori_loop(0, 16, one, jnp.zeros((8, 128), f32))

    adam0 = adam_m(0)
    adam1 = adam_m(1)
    mn_out = pltpu.make_async_copy(mn, mn_hbm, osem.at[0])
    mn_out.start()

    def split(src, hi, lo):
        def one(i, carry):
            for s in range(SLOTS):
                v = src[s, i // NZ, i % NZ]
                h = v.astype(jnp.bfloat16)
                hi[s, i // NZ, i % NZ] = h
                lo[s, i // NZ, i % NZ] = (v - h.astype(f32)).astype(jnp.bfloat16)
            return carry
        lax.fori_loop(0, NX * NZ, one, 0)

    loads[0].wait()
    split(rf, rhi, rlo)
    loads[2].wait()
    split(lf, lhi, llo)
    loads[3].wait()

    def whole(ref, s):
        return ref[s].reshape(B, B)

    def xsend(d):
        zst[...] = zin[d]
        for j in range(LINE):
            for s in range(SLOTS):
                piece = zst[tab[o_deal + j * SLOTS + s]]
                if j:
                    xout[d, j, s] = piece
                else:
                    xin[d, j, s] = piece
            if j:
                pltpu.make_async_remote_copy(src_ref=xout.at[d, j], dst_ref=xin.at[d, j], send_sem=xs,
                                             recv_sem=xr.at[d], device_id=xdev(j), device_id_type=MESH).start()

    def tchunk(d):
        pltpu.make_async_copy(xin.at[d, pl.ds(1, LINE - 1)], xin.at[d, pl.ds(1, LINE - 1)], xr.at[d]).wait()
        zsrc = lax.rem(z - d + NZ, NZ)
        for s in range(SLOTS):
            rows = []
            for dx in range(NX):
                p0 = xin[d, dx * NC + c, s].astype(f32)
                p1 = xin[d, dx * NC + (1 - c), s].astype(f32)
                lft = jnp.concatenate([p0[:8], p1[:8]], axis=0)
                rgt = jnp.concatenate([p0[8:], p1[8:]], axis=0)
                rows.append(jnp.concatenate([lft, rgt], axis=1).astype(jnp.bfloat16))
            a = jnp.concatenate(rows, axis=0)
            t = jnp.dot(a, whole(rhi, s), preferred_element_type=f32) + jnp.dot(a, whole(rlo, s), preferred_element_type=f32)
            h = t.astype(jnp.bfloat16)
            lo = (t - h.astype(f32)).astype(jnp.bfloat16)
            for dx in range(NX):
                xsrc = lax.rem(x - dx + NX, NX)
                thi[s, xsrc, zsrc] = h[dx * 16:(dx + 1) * 16]
                tlo[s, xsrc, zsrc] = lo[dx * 16:(dx + 1) * 16]

    xsend(0)

    def forward(k, carry):
        d = offset_of(k)
        pltpu.make_async_copy(zin.at[d], zin.at[d], zr.at[d]).wait()
        xsend(d)
        tchunk(offset_of(k - 1))
        return carry

    lax.fori_loop(1, NZ, forward, 0)
    tchunk(offset_of(NZ - 1))

    lane = lax.broadcasted_iota(jnp.int32, (8, 128), 1)
    row = lax.broadcasted_iota(jnp.int32, (8, 128), 0)
    base = (x * NC + c) * SLOTS
    nrm[...] = jnp.zeros_like(nrm)
    per = NZ // np_groups

    def pgroup(n):
        for s in range(SLOTS):
            hs, ls = [], []
            for i in range(per):
                zz = lax.rem(z + offset_of((n * per + i + 1) % NZ), NZ)
                hs.append(lhi[s, :, zz].reshape(64, B))
                ls.append(llo[s, :, zz].reshape(64, B))
            h = jnp.concatenate(hs, axis=0)
            lo = jnp.concatenate(ls, axis=0)
            p = jnp.dot(h, whole(thi, s), preferred_element_type=f32)
            p = p + jnp.dot(h, whole(tlo, s), preferred_element_type=f32)
            p = p + jnp.dot(lo, whole(thi, s), preferred_element_type=f32)
            pbuf[s] = p

        def quant(i, carry):
            d = offset_of((n * per + i + 1) % NZ)
            sums = [jnp.zeros((8, 128), f32) for _ in range(SLOTS)]
            for xd in range(NX):
                for cd in range(NC):
                    j = lax.rem(xd - x + NX, NX) * NC + lax.rem(cd + c, NC)
                    lev = jnp.zeros((8, 128), jnp.int32)
                    at = pl.multiple_of(i * 64 + (xd * NC + cd) * 8, 8)
                    for s in range(SLOTS):
                        v = pbuf[s, pl.ds(at, 8), :]
                        sq = v * v
                        sums[s] = sums[s] + ((sq[:, :128] + sq[:, 128:256]) + (sq[:, 256:384] + sq[:, 384:]))
                        top = jnp.maximum(jnp.max(jnp.abs(v), axis=1, keepdims=True), 1e-30)
                        level = jnp.ceil(jnp.log2(top) * STEPS) + 1.0
                        q = jnp.round(v * (jnp.exp2(level * (-1.0 / STEPS)) * 32767.0)).astype(jnp.int32)
                        packed = (q[:, :256] << 16) | (q[:, 256:] & 0xFFFF)
                        xrout[d, j, 2 * s] = packed[:, :128]
                        xrout[d, j, 2 * s + 1] = packed[:, 128:]
                        lev = jnp.where(lane == base + s, level.astype(jnp.int32), lev)
                    xrout[d, j, 2 * SLOTS] = lev
            for s in range(SLOTS):
                which = tab[o_mine + s]
                nrm[0] += jnp.where(which == 1, sums[s], 0.0)
                nrm[1] += jnp.where(which == 2, sums[s], 0.0)
            xrin[d, 0] = xrout[d, 0]
            for j in range(1, LINE):
                pltpu.make_async_remote_copy(src_ref=xrout.at[d, j], dst_ref=xrin.at[d, j], send_sem=xrs,
                                             recv_sem=xrr.at[d], device_id=xdev(j), device_id_type=MESH).start()
            return carry

        lax.fori_loop(0, per, quant, 0)

    def relay(k):
        d = offset_of(k % NZ)
        pltpu.make_async_copy(xrin.at[d, pl.ds(1, LINE - 1)], xrin.at[d, pl.ds(1, LINE - 1)], xrr.at[d]).wait()

        def put(dst):
            for j in range(LINE):
                for s in range(SLOTS):
                    xst[j * SLOTS + s, 0] = xrin[d, j, 2 * s]
                    xst[j * SLOTS + s, 1] = xrin[d, j, 2 * s + 1]

            def one(p, carry):
                code = tab[o_col + p]
                dst[d, 2 * p] = xst[code, 0]
                dst[d, 2 * p + 1] = xst[code, 1]
                return carry
            lax.fori_loop(0, cap, one, 0, unroll=6)
            lev = xrin[d, 0, 2 * SLOTS]
            for j in range(1, LINE):
                lev = lev + xrin[d, j, 2 * SLOTS]
            dst[d, 2 * cap] = lev
        return d, put

    def relay_out(k, carry):
        d, put = relay(k)
        put(zrout)
        pltpu.make_async_remote_copy(src_ref=zrout.at[d], dst_ref=zrin.at[d], send_sem=zrs, recv_sem=zrr.at[d],
                                     device_id=zdev(d), device_id_type=MESH).start()
        return carry

    pgroup(0)

    def back(n, carry):
        pgroup(n)
        lax.fori_loop((n - 1) * per + 1, n * per + 1, relay_out, 0)
        return carry

    if np_groups > 1:
        lax.fori_loop(1, np_groups, back, 0)

    def pack_row(i, v):
        return jnp.where(row == i, jnp.sum(v, axis=0, keepdims=True), 0.0)

    over = jnp.where(tab[o_over] > 0, 1.0, 0.0)
    local = pack_row(0, adam0) + pack_row(1, adam1) + pack_row(2, nrm[0]) + pack_row(3, nrm[1])
    tot[0] = local + jnp.where(row == 4, over, 0.0)

    def share(stage, devs, base_at):
        for i, dev in enumerate(devs):
            pltpu.make_async_remote_copy(src_ref=tot.at[stage], dst_ref=nin.at[base_at + i], send_sem=ns.at[stage],
                                         recv_sem=nr.at[stage], device_id=dev, device_id_type=MESH).start()

    def gather(stage, count, base_at):
        view = nin.at[pl.ds(base_at, count)]
        pltpu.make_async_copy(view, view, nr.at[stage]).wait()
        acc = tot[stage]
        for i in range(count):
            acc = acc + nin[base_at + i]
        return acc

    share(0, [xdev(j) for j in range(1, LINE)], 0)
    lax.fori_loop((np_groups - 1) * per + 1, NZ, relay_out, 0)
    d, put = relay(NZ)
    put(zrin)
    tot[1] = gather(0, LINE - 1, 0)
    share(1, [zdev(d) for d in range(1, NZ)], 7)
    tot[2] = gather(1, NZ - 1, 7)
    share(2, [rdev(i) for i in range(1, NREP)], 14)
    total = gather(2, NREP - 1, 14)
    stat_ref[...] = total
    sums = jnp.sum(total, axis=1, keepdims=True)
    scale = jnp.sqrt(sums[0:2]) / (jnp.sqrt(sums[2:4]) + 1e-6) * (1.0 / 32767.0)

    view = zrin.at[pl.ds(1, NZ - 1)]

    def landed(d, carry):
        pltpu.make_async_copy(zrin.at[d], zrin.at[d], zrr.at[d]).wait()
        return carry

    lax.fori_loop(1, NZ, landed, 0)

    def finish(m):
        factor = scale[m:m + 1]

        def one(k, carry):
            i = m * 16 + k
            for q in range(3):
                b = i * 3 + q
                d, p, e = tab[o_fd + b], tab[o_fp + b], tab[o_fe + b]
                lev = jnp.sum(jnp.where(lane == e, zrin[d, 2 * cap], 0).astype(f32), axis=1, keepdims=True)
                mul = jnp.exp2(lev * (1.0 / STEPS)) * factor
                for h in range(2):
                    w = zrin[d, 2 * p + h]
                    for u, v in ((0, w >> 16), (1, (w << 16) >> 16)):
                        cols = pl.ds(q * B + u * 256 + h * 128, 128)
                        mom[i, :, cols] = 0.9 * mom[i, :, cols] + v.astype(f32) * mul
            return carry

        lax.fori_loop(0, 16, one, 0, unroll=2)
        half = pl.ds(m * 16, 16)
        cp = pltpu.make_async_copy(mom.at[half], out_hbm.at[half], osem.at[1 + m])
        cp.start()
        return cp

    outs = [finish(0), finish(1)]

    def sent(ref, sem):
        pltpu.make_async_copy(ref, ref, sem).wait()

    sent(zout.at[pl.ds(1, NZ - 1)], zs)
    sent(xout.at[:, pl.ds(1, LINE - 1)], xs)
    sent(xrout.at[:, pl.ds(1, LINE - 1)], xrs)
    sent(zrout.at[pl.ds(1, NZ - 1)], zrs)
    sent(nin.at[pl.ds(0, 7)], ns.at[0])
    sent(nin.at[pl.ds(7, 7)], ns.at[1])
    sent(nin.at[pl.ds(14, 3)], ns.at[2])
    mn_out.wait()
    for cp in outs:
        cp.wait()


def fused(grads, second_moment, momentum, left, right, owner, slot, cap, cid):
    table, offs = tables(owner, slot, cap)
    bf16, f32, i32 = jnp.bfloat16, jnp.float32, jnp.int32
    np_groups = 4
    rows = 64 * (NZ // np_groups)
    fac = (SLOTS, NX, NZ, 16, B)
    v, dma = pltpu.VMEM, pltpu.SemaphoreType.DMA
    hbm, vm, sm = (pl.BlockSpec(memory_space=s) for s in (pl.ANY, pltpu.VMEM, pltpu.SMEM))
    flat = (32, 8, 3 * B)
    return pl.pallas_call(
        functools.partial(kernel, cap, offs, np_groups),
        out_shape=(
            jax.ShapeDtypeStruct(flat, f32),
            jax.ShapeDtypeStruct(flat, f32),
            jax.ShapeDtypeStruct((8, 128), f32),
        ),
        in_specs=[sm, vm, hbm, hbm, hbm, hbm],
        out_specs=(hbm, hbm, vm),
        scratch_shapes=[
            v((NBLK, 16, 256), bf16), v(flat, f32), v(flat, f32), v(flat, f32),
            v(fac, f32), v(fac, f32), v(fac, bf16), v(fac, bf16), v(fac, bf16), v(fac, bf16),
            v(fac, bf16), v(fac, bf16), v((SLOTS, rows, B), f32),
            v((NZ, cap, 16, 256), bf16), v((NZ, cap, 16, 256), bf16),
            v((NZ, LINE, SLOTS, 16, 256), bf16), v((NZ, LINE, SLOTS, 16, 256), bf16),
            v((NZ, LINE, 2 * SLOTS + 1, 8, 128), i32), v((NZ, LINE, 2 * SLOTS + 1, 8, 128), i32),
            v((NZ, 2 * cap + 1, 8, 128), i32), v((NZ, 2 * cap + 1, 8, 128), i32),
            v((cap, 16, 256), bf16), v((PLACES, 2, 8, 128), i32),
            v((2, 8, 128), f32), v((17, 8, 128), f32), v((3, 8, 128), f32),
            dma((4,)), dma((3,)), dma, dma((NZ,)), dma, dma((NZ,)), dma, dma((NZ,)), dma, dma((NZ,)),
            dma((3,)), dma((3,)),
        ],
        compiler_params=pltpu.CompilerParams(
            collective_id=cid, has_side_effects=True, vmem_limit_bytes=56 * 2**20
        ),
        cost_estimate=pl.CostEstimate(flops=4 * 10**9, bytes_accessed=14 * 10**6, transcendentals=0),
    )(
        table,
        grads.reshape(flat),
        second_moment.reshape(flat),
        momentum.reshape(flat),
        left.reshape(fac),
        right.reshape(fac),
    )


def shards(grads, second_moment, momentum, left_inverse_root, right_root, owner, slot):
    new, mom, stat = fused(
        grads, second_moment, momentum, left_inverse_root, right_root, owner[0], slot[0], CAP, 0
    )
    return new.reshape(second_moment.shape), mom.reshape(momentum.shape)


def solution(mesh):
    in_specs = (
        P(None, None, "fsdp", "rep"),
        P(None, None, "fsdp", "rep"),
        P(None, None, "fsdp", "rep"),
        P("rep", "fsdp", None, None, None),
        P("rep", "fsdp", None, None, None),
        P("rep", None),
        P("rep", None),
    )
    out_specs = (P(None, None, "fsdp", "rep"), P(None, None, "fsdp", "rep"))
    return jax.shard_map(shards, mesh=mesh, in_specs=in_specs, out_specs=out_specs, check_vma=False)
```

```python
import functools

import jax
import jax.numpy as jnp
from jax import lax
from jax.experimental import pallas as pl
from jax.experimental.pallas import tpu as pltpu
from jax.sharding import PartitionSpec as P

MESH = pl.DeviceIdType.MESH
NX, NZ, NC, NREP = 4, 8, 2, 4
LINE = NX * NC
SLOTS = 3
B = 512
NBLK = 96
PLACES = LINE * SLOTS
CAP = 19
GROUPS = 4
LAG_A = 3
LAG_B = 4
ALLP = False
EARLY = 5
FLAT = (32, 8, 1536)
T_DEAL, T_COLLECT, T_MINE, T_FIN = 8, 9, 10, 11
STEPS = 16.0


def offset_of(k):
    return jnp.where(k % 2 == 1, (k + 1) // 2, (NZ - k // 2) % NZ)


def within(i, n):
    return jnp.minimum(jnp.maximum(i, 0), n - 1)


def build_tables(owner, slot, x, z, c, cap):
    i32, f32 = jnp.int32, jnp.float32
    sq = (NBLK, NBLK)
    eye = lax.broadcasted_iota(i32, sq, 0) == lax.broadcasted_iota(i32, sq, 1)

    def column(v):
        wide = jnp.broadcast_to(v.astype(f32), sq)
        return jnp.sum(jnp.where(eye, wide, 0.0), axis=1, keepdims=True)

    line = (owner >> 1) & (NZ - 1)
    ox, oc = owner >> 4, owner & 1
    place = slot * LINE + ox * NC + oc
    linef, placef = line.astype(f32), place.astype(f32)
    line_col, place_col = column(line), column(place)
    before = (jnp.broadcast_to(line_col, sq) == jnp.broadcast_to(linef, sq)) & (
        jnp.broadcast_to(place_col, sq) < jnp.broadcast_to(placef, sq))
    rank = jnp.sum(jnp.where(before, 1.0, 0.0), axis=0, keepdims=True)
    rank_col = column(rank)
    firsts = (jnp.broadcast_to(line_col, sq) == jnp.broadcast_to(linef, sq)) & (
        jnp.broadcast_to(place_col, sq) < float(LINE))
    spare = jnp.maximum(EARLY - jnp.sum(jnp.where(firsts, 1.0, 0.0), axis=0, keepdims=True), 0.0)
    seat = jnp.where((slot == 0) & (rank < float(EARLY)), rank, rank + spare)
    seat_col = column(seat)
    code_col = column(slot * LINE + ((x - ox) & (NX - 1)) * NC + ((oc + c) & 1))
    block_col = lax.broadcasted_iota(i32, (NBLK, 128), 0).astype(f32)
    lane = lax.broadcasted_iota(i32, (NBLK, 128), 1)
    wide = (NBLK, 128)
    line_w, place_w, rank_w, code_w, seat_w = (
        jnp.broadcast_to(v, wide) for v in (line_col, place_col, rank_col, code_col, seat_col))
    lanef = lane.astype(f32)

    def pick(match, value):
        return jnp.sum(jnp.where(match, value, 0.0), axis=0, keepdims=True)

    at_pos = rank_w == lanef
    most = float(NBLK - 1)
    rows = [jnp.minimum(pick(at_pos & (line_w == ((z + d) & (NZ - 1)).astype(f32)), block_col), most) for d in range(NZ)]
    here = line_w == z.astype(f32)
    j = lane & (LINE - 1)
    dealt = ((lane - j) + ((x + (j >> 1)) & (NX - 1)) * NC + ((c + j) & 1)).astype(f32)
    rows.append(jnp.minimum(pick(here & (place_w == dealt), rank_w), cap - 1.0))
    rows.append(jnp.minimum(pick(here & (seat_w == lanef), code_w), PLACES - 1.0))
    mine = (x * NC + c + lane * LINE).astype(f32)
    rows.append(pick(here & (place_w == mine), jnp.where(block_col >= NBLK // 2, 2.0, 1.0)))
    finals = [(z - line) & (NZ - 1), jnp.minimum(seat, cap - 1.0).astype(i32), (ox * NC + oc) * SLOTS + slot]
    top = jnp.max(seat, axis=1, keepdims=True)
    return [r.astype(i32) for r in rows], finals, top


def kernel(cap, per, owner_ref, slot_ref, g_ref, sm_hbm, left_hbm, right_hbm,
           mn_hbm, zr_hbm, stat_ref, tabv,
           tab, gp, sm, mn, lf, rf, lhi, llo, rhi, rlo, thi, tlo, pbuf,
           zout, zin, xout_a, xin_a, xout_b, xin_b, xr_a, xi_a, xr_b, xi_b, zrout, zrin, zst, xst, lev0, nrm, nin, tot,
           lsem, osem, zs, zr_a, zr_b, xs_a, xs_b, xw_a, xw_b, xrs_a, xrs_b, xrw_a, xrw_b, zrs, zrw_a, zrw_b, ns, nr):
    f = lax.axis_index("fsdp")
    r = lax.axis_index("rep")
    x, z, c = f // (NZ * NC), (f // NC) % NZ, f % NC
    f32, bf16 = jnp.float32, jnp.bfloat16

    def zdev(d):
        return (x * (NZ * NC) + lax.rem(z + d, NZ) * NC + c, r)

    def xdev(j):
        return (lax.rem(x + j // NC, NX) * (NZ * NC) + z * NC + lax.rem(c + j % NC, NC), r)

    def rdev(i):
        return (f, lax.rem(r + i, NREP))

    def push(src, dst, ssem, rsem, dev):
        pltpu.make_async_remote_copy(src_ref=src, dst_ref=dst, send_sem=ssem, recv_sem=rsem,
                                     device_id=dev, device_id_type=MESH).start()

    def done(ref, sem):
        pltpu.make_async_copy(ref, ref, sem).wait()

    peers = [zdev(d) for d in range(1, NZ)] + [xdev(j) for j in range(1, LINE)] + [rdev(i) for i in range(1, NREP)]
    bar = pltpu.get_barrier_semaphore()
    for dev in peers:
        pl.semaphore_signal(bar, 1, device_id=dev, device_id_type=MESH)

    loads = [
        pltpu.make_async_copy(right_hbm, rf, lsem.at[0]),
        pltpu.make_async_copy(left_hbm, lf, lsem.at[2]),
        pltpu.make_async_copy(sm_hbm, sm, lsem.at[1]),
    ]
    for cp in loads:
        cp.start()

    rows, finals, top = build_tables(owner_ref[...], slot_ref[...], x, z, c, cap)
    for i, v in enumerate(rows):
        tabv[pl.ds(i, 1), :] = v
    for i, v in enumerate(finals):
        tabv[pl.ds(T_FIN + i, 1), :] = jnp.zeros((1, 128), jnp.int32)
        tabv[pl.ds(T_FIN + i, 1), pl.ds(0, NBLK)] = v
    tabv[pl.ds(T_FIN + 3, 2), :] = jnp.zeros((2, 128), jnp.int32)
    over = jnp.where(top >= cap, 1.0, 0.0)
    tcopy = pltpu.make_async_copy(tabv, tab, lsem.at[3])
    tcopy.start()

    def repack(i, carry):
        row = g_ref[i].astype(f32)
        for q in range(3):
            a = row[:, q * B:q * B + B // 2]
            b = row[:, q * B + B // 2:(q + 1) * B]
            gp[i * 3 + q] = jnp.concatenate([a, b], axis=0).astype(bf16)
        return carry

    lax.fori_loop(0, 32, repack, 0)
    tcopy.wait()

    def fill(d, dst, lo, hi):
        for p in range(lo, hi):
            dst[d, p] = gp[within(tab[d, p], NBLK)]

    part_a, part_b = pl.ds(0, LINE), pl.ds(LINE, cap - LINE)

    def zsend_a(k, carry):
        d = offset_of(k)
        fill(d, zout, 0, LINE)

        @pl.when(k == 1)
        def _():
            pl.semaphore_wait(bar, len(peers))

        push(zout.at[d, part_a], zin.at[d, part_a], zs, zr_a.at[d], zdev(d))
        return carry

    def zsend_b(k, carry):
        d = offset_of(k)
        fill(d, zout, LINE, cap)
        push(zout.at[d, part_b], zin.at[d, part_b], zs, zr_b.at[d], zdev(d))
        return carry

    lax.fori_loop(1, NZ, zsend_a, 0)
    lax.fori_loop(1, NZ, zsend_b, 0)
    fill(0, zin, 0, cap)

    def split(src, hi, lo):
        def one(i, carry):
            for s in range(SLOTS):
                v = src[s, i // NZ, i % NZ]
                h = v.astype(bf16)
                hi[s, i // NZ, i % NZ] = h
                lo[s, i // NZ, i % NZ] = (v - h.astype(f32)).astype(bf16)
            return carry
        lax.fori_loop(0, NX * NZ, one, 0)

    loads[0].wait()
    split(rf, rhi, rlo)
    loads[1].wait()
    split(lf, lhi, llo)

    def whole(ref, s):
        return ref[s].reshape(B, B)

    def tiles(d, s, piece):
        zsrc = lax.rem(z - d + NZ, NZ)
        blocks = []
        for dx in range(NX):
            p0 = piece(dx * NC + c).astype(f32)
            p1 = piece(dx * NC + (1 - c)).astype(f32)
            lft = jnp.concatenate([p0[:8], p1[:8]], axis=0)
            rgt = jnp.concatenate([p0[8:], p1[8:]], axis=0)
            blocks.append(jnp.concatenate([lft, rgt], axis=1).astype(bf16))
        a = jnp.concatenate(blocks, axis=0)
        t = jnp.dot(a, whole(rhi, s), preferred_element_type=f32) + jnp.dot(a, whole(rlo, s), preferred_element_type=f32)
        h = t.astype(bf16)
        lo = (t - h.astype(f32)).astype(bf16)
        for dx in range(NX):
            xsrc = lax.rem(x - dx + NX, NX)
            thi[s, xsrc, zsrc] = h[dx * 16:(dx + 1) * 16]
            tlo[s, xsrc, zsrc] = lo[dx * 16:(dx + 1) * 16]

    others = pl.ds(1, LINE - 1)

    def xsend_a(d):
        zst[pl.ds(0, LINE)] = zin[d, pl.ds(0, LINE)]
        for j in range(LINE):
            piece = zst[within(tab[T_DEAL, j], LINE)]
            if j:
                xout_a[d, j] = piece
                push(xout_a.at[d, j], xin_a.at[d, j], xs_a, xw_a.at[d], xdev(j))
            else:
                xin_a[d, 0] = piece

    def tchunk_a(d):
        done(xin_a.at[d, others], xw_a.at[d])
        tiles(d, 0, lambda j: xin_a[d, j])

    def xsend_b(d):
        zst[...] = zin[d]
        for j in range(LINE):
            for s in (1, 2):
                piece = zst[within(tab[T_DEAL, s * LINE + j], cap)]
                if j:
                    xout_b[d, j, s - 1] = piece
                else:
                    xin_b[d, 0, s - 1] = piece
            if j:
                push(xout_b.at[d, j], xin_b.at[d, j], xs_b, xw_b.at[d], xdev(j))

    def tchunk_b(d):
        done(xin_b.at[d, others], xw_b.at[d])
        for s in (1, 2):
            tiles(d, s, lambda j, s=s: xin_b[d, j, s - 1])

    xsend_a(0)

    def forward_a(k, carry):
        d = offset_of(k)
        done(zin.at[d, part_a], zr_a.at[d])
        xsend_a(d)

        @pl.when(k >= LAG_A)
        def _():
            tchunk_a(offset_of(k - LAG_A))
        return carry

    lax.fori_loop(1, NZ, forward_a, 0)
    lax.fori_loop(NZ - LAG_A, NZ, lambda k, carry: (tchunk_a(offset_of(k)), carry)[1], 0)

    lane = lax.broadcasted_iota(jnp.int32, (8, 128), 1)
    row = lax.broadcasted_iota(jnp.int32, (8, 128), 0)
    base = (x * NC + c) * SLOTS
    nrm[...] = jnp.zeros_like(nrm)

    def back_of(i):
        return offset_of(NZ - 1 - i)

    def product(s, first, count):
        hs, ls = [], []
        for i in range(count):
            zz = lax.rem(z + back_of(first + i), NZ)
            hs.append(lhi[s, :, zz].reshape(64, B))
            ls.append(llo[s, :, zz].reshape(64, B))
        h = jnp.concatenate(hs, axis=0)
        lo = jnp.concatenate(ls, axis=0)
        p = jnp.dot(h, whole(thi, s), preferred_element_type=f32)
        p = p + jnp.dot(h, whole(tlo, s), preferred_element_type=f32)
        return p + jnp.dot(lo, whole(thi, s), preferred_element_type=f32)

    def code_rows(v):
        top = jnp.maximum(jnp.max(jnp.abs(v), axis=1, keepdims=True), 1e-30)
        level = jnp.ceil(jnp.log2(top) * STEPS) + 1.0
        q = jnp.round(v * (jnp.exp2(level * (-1.0 / STEPS)) * 32767.0)).astype(jnp.int32)
        packed = (q[:, :256] << 16) | (q[:, 256:] & 0xFFFF)
        sq = v * v
        return packed, level.astype(jnp.int32), (sq[:, :128] + sq[:, 128:256]) + (sq[:, 256:384] + sq[:, 384:])

    def tally(s, v):
        which = tab[T_MINE, s]
        nrm[0] += jnp.where(which == 1, v, 0.0)
        nrm[1] += jnp.where(which == 2, v, 0.0)

    def target(xd, cd):
        return lax.rem(xd - x + NX, NX) * NC + lax.rem(cd + c, NC)

    pbuf[0] = product(0, 0, NZ)

    def code_a(i, carry):
        d = back_of(i)
        total = jnp.zeros((8, 128), f32)
        for xd in range(NX):
            for cd in range(NC):
                j = target(xd, cd)
                v = pbuf[0, pl.ds(pl.multiple_of(i * 64 + (xd * NC + cd) * 8, 8), 8), :]
                packed, level, sq = code_rows(v)
                total = total + sq
                xr_a[d, j, 0] = packed[:, :128]
                xr_a[d, j, 1] = packed[:, 128:]
                lev0[d, j] = jnp.where(lane == base, level, 0)
        tally(0, total)
        xi_a[d, 0] = xr_a[d, 0]
        for j in range(1, LINE):
            push(xr_a.at[d, j], xi_a.at[d, j], xrs_a, xrw_a.at[d], xdev(j))
        return carry

    lax.fori_loop(0, NZ, code_a, 0)

    loads[2].wait()

    def adam_m(m):
        def one(k, acc):
            i = m * 16 + k
            g = g_ref[i].astype(f32)
            new = 0.9 * sm[i] + 0.1 * g * g
            mn[i] = new
            a = g / (jnp.sqrt(new) + 1e-8)
            a = a * a
            for q in range(12):
                acc = acc + a[:, q * 128:(q + 1) * 128]
            return acc
        return lax.fori_loop(0, 16, one, jnp.zeros((8, 128), f32))

    adam0 = adam_m(0)
    adam1 = adam_m(1)
    mn_out = pltpu.make_async_copy(mn, mn_hbm, osem.at[0])
    mn_out.start()

    seats_a, seats_b = pl.ds(0, 2 * EARLY), pl.ds(2 * EARLY, 2 * (cap - EARLY) + 1)

    def stage_a(d):
        for j in range(LINE):
            xst[j] = xi_a[d, j]

    def seat(dst, d, lo, hi):
        for p in range(lo, hi):
            code = within(tab[T_COLLECT, p], PLACES)
            dst[d, 2 * p] = xst[code, 0]
            dst[d, 2 * p + 1] = xst[code, 1]

    def relay_a(i, dst):
        d = back_of(i)
        done(xi_a.at[d, others], xrw_a.at[d])
        stage_a(d)
        seat(dst, d, 0, EARLY)

    def zback_a(i, carry):
        d = back_of(i)
        push(zrout.at[d, seats_a], zrin.at[d, seats_a], zrs, zrw_a.at[d], zdev(d))
        return carry

    xsend_b(0)

    def forward_b(k, carry):
        d = offset_of(k)
        relay_a(k - 1, zrout)
        done(zin.at[d, part_b], zr_b.at[d])
        xsend_b(d)

        @pl.when(k == NZ - 1)
        def _():
            lax.fori_loop(0, NZ - 1, zback_a, 0)

        @pl.when(k >= LAG_B)
        def _():
            tchunk_b(offset_of(k - LAG_B))
        return carry

    lax.fori_loop(1, NZ, forward_b, 0)
    lax.fori_loop(NZ - LAG_B, NZ, lambda k, carry: (tchunk_b(offset_of(k)), carry)[1], 0)

    def pgroup(n):
        for s in (1, 2):
            pbuf[s, pl.ds(0, 64 * per), :] = product(s, n * per, per)

        def code_b(i, carry):
            d = back_of(n * per + i)
            totals = [jnp.zeros((8, 128), f32) for _ in range(2)]
            for xd in range(NX):
                for cd in range(NC):
                    j = target(xd, cd)
                    lev = lev0[d, j]
                    at = pl.ds(pl.multiple_of(i * 64 + (xd * NC + cd) * 8, 8), 8)
                    for s in (1, 2):
                        packed, level, sq = code_rows(pbuf[s, at, :])
                        totals[s - 1] = totals[s - 1] + sq
                        xr_b[d, j, 2 * s - 2] = packed[:, :128]
                        xr_b[d, j, 2 * s - 1] = packed[:, 128:]
                        lev = jnp.where(lane == base + s, level, lev)
                    xr_b[d, j, 4] = lev
            tally(1, totals[0])
            tally(2, totals[1])
            xi_b[d, 0] = xr_b[d, 0]
            for j in range(1, LINE):
                push(xr_b.at[d, j], xi_b.at[d, j], xrs_b, xrw_b.at[d], xdev(j))
            return carry

        lax.fori_loop(0, per, code_b, 0)

    def relay_b(i, dst):
        d = back_of(i)
        done(xi_b.at[d, others], xrw_b.at[d])
        stage_a(d)
        lev = xi_b[d, 0, 4]
        for j in range(LINE):
            xst[LINE + j] = xi_b[d, j, pl.ds(0, 2)]
            xst[2 * LINE + j] = xi_b[d, j, pl.ds(2, 2)]
            if j:
                lev = lev + xi_b[d, j, 4]
        dst[d, 2 * cap] = lev
        seat(dst, d, EARLY, cap)
        return d

    def relay_out(i, carry):
        d = relay_b(i, zrout)
        push(zrout.at[d, seats_b], zrin.at[d, seats_b], zrs, zrw_b.at[d], zdev(d))
        return carry

    pgroup(0)
    groups = NZ // per

    def back(n, carry):
        pgroup(n)
        if not ALLP:
            lax.fori_loop((n - 1) * per, n * per, relay_out, 0)
        return carry

    lax.fori_loop(1, groups, back, 0)

    def pack_row(i, v):
        return jnp.where(row == i, jnp.sum(v, axis=0, keepdims=True), 0.0)

    local = pack_row(0, adam0) + pack_row(1, adam1) + pack_row(2, nrm[0]) + pack_row(3, nrm[1])
    tot[0] = local + jnp.where(row == 4, over, 0.0)

    def share(stage, devs, base_at):
        for i, dev in enumerate(devs):
            push(tot.at[stage], nin.at[base_at + i], ns.at[stage], nr.at[stage], dev)

    def gather(stage, count, base_at):
        done(nin.at[pl.ds(base_at, count)], nr.at[stage])
        acc = tot[stage]
        for i in range(count):
            acc = acc + nin[base_at + i]
        return acc

    share(0, [xdev(j) for j in range(1, LINE)], 0)
    lax.fori_loop(0 if ALLP else (groups - 1) * per, NZ - 1, relay_out, 0)
    relay_a(NZ - 1, zrin)
    relay_b(NZ - 1, zrin)
    tot[1] = gather(0, LINE - 1, 0)
    share(1, [zdev(d) for d in range(1, NZ)], 7)
    tot[2] = gather(1, NZ - 1, 7)
    share(2, [rdev(i) for i in range(1, NREP)], 14)
    total = gather(2, NREP - 1, 14)
    stat_ref[...] = total

    def landed(d, carry):
        done(zrin.at[d, seats_a], zrw_a.at[d])
        done(zrin.at[d, seats_b], zrw_b.at[d])
        return carry

    lax.fori_loop(1, NZ, landed, 0)
    zr_out = pltpu.make_async_copy(zrin, zr_hbm, osem.at[1])
    zr_out.start()

    done(zout.at[pl.ds(1, NZ - 1)], zs)
    done(xout_a.at[:, others], xs_a)
    done(xout_b.at[:, others], xs_b)
    done(xr_a.at[:, others], xrs_a)
    done(xr_b.at[:, others], xrs_b)
    done(zrout.at[pl.ds(1, NZ - 1)], zrs)
    done(nin.at[pl.ds(0, 7)], ns.at[0])
    done(nin.at[pl.ds(7, 7)], ns.at[1])
    done(nin.at[pl.ds(14, 3)], ns.at[2])
    mn_out.wait()
    zr_out.wait()


def finish(cap, tab, zin, total, mn_hbm, mom_hbm, mn_out, out_hbm, mom, mn, osem, lsem):
    parts = 4
    per = 32 // parts
    loads = []
    for i in range(parts):
        view = pl.ds(i * per, per)
        loads.append(pltpu.make_async_copy(mom_hbm.at[view], mom.at[view], lsem.at[i]))
        loads[-1].start()
    fetch = pltpu.make_async_copy(mn_hbm, mn, lsem.at[parts])
    fetch.start()
    copy = pltpu.make_async_copy(mn, mn_out, osem.at[parts])
    sums = jnp.sum(total[...], axis=1, keepdims=True)
    scale = jnp.sqrt(sums[0:2]) / (jnp.sqrt(sums[2:4]) + 1e-6) * (1.0 / 32767.0)
    lane = lax.broadcasted_iota(jnp.int32, (8, 128), 1)
    outs = []
    for n in range(parts):
        m = n * 2 // parts
        factor = scale[m:m + 1]

        def one(k, carry):
            i = n * per + k
            for q in range(3):
                b = i * 3 + q
                d, p, e = tab[T_FIN, b], tab[T_FIN + 1, b], tab[T_FIN + 2, b]
                lev = jnp.sum(jnp.where(lane == e, zin[d, 2 * cap], 0).astype(jnp.float32), axis=1, keepdims=True)
                mul = jnp.exp2(lev * (1.0 / STEPS)) * factor
                for h in range(2):
                    w = zin[d, 2 * p + h]
                    for u, v in ((0, w >> 16), (1, (w << 16) >> 16)):
                        cols = pl.ds(q * B + u * 256 + h * 128, 128)
                        mom[i, :, cols] = 0.9 * mom[i, :, cols] + v.astype(jnp.float32) * mul
            return carry

        loads[n].wait()
        lax.fori_loop(0, per, one, 0, unroll=4)
        view = pl.ds(n * per, per)
        outs.append(pltpu.make_async_copy(mom.at[view], out_hbm.at[view], osem.at[n]))
        outs[-1].start()
        if n == 0:
            fetch.wait()
            copy.start()
    copy.wait()
    for cp in outs:
        cp.wait()


def spaces():
    return (pl.BlockSpec(memory_space=s) for s in (pl.ANY, pltpu.VMEM, pltpu.SMEM))


def fused(grads, second_moment, left, right, owner, slot, cap, cid):
    bf16, f32, i32 = jnp.bfloat16, jnp.float32, jnp.int32
    fac = (SLOTS, NX, NZ, 16, B)
    v, dma = pltpu.VMEM, pltpu.SemaphoreType.DMA
    hbm, vm, sm = spaces()
    tiles = (NZ, 2 * cap + 1, 8, 128)
    return pl.pallas_call(
        functools.partial(kernel, cap, NZ // GROUPS),
        out_shape=(
            jax.ShapeDtypeStruct(FLAT, f32),
            jax.ShapeDtypeStruct(tiles, i32),
            jax.ShapeDtypeStruct((8, 128), f32),
            jax.ShapeDtypeStruct((16, 128), i32),
        ),
        in_specs=[vm, vm, vm, hbm, hbm, hbm],
        out_specs=(hbm, hbm, vm, vm),
        scratch_shapes=[
            pltpu.SMEM((16, 128), i32),
            v((NBLK, 16, 256), bf16), v(FLAT, f32), v(FLAT, f32),
            v(fac, f32), v(fac, f32), v(fac, bf16), v(fac, bf16), v(fac, bf16), v(fac, bf16),
            v(fac, bf16), v(fac, bf16), v((SLOTS, B, B), f32),
            v((NZ, cap, 16, 256), bf16), v((NZ, cap, 16, 256), bf16),
            v((NZ, LINE, 16, 256), bf16), v((NZ, LINE, 16, 256), bf16),
            v((NZ, LINE, 2, 16, 256), bf16), v((NZ, LINE, 2, 16, 256), bf16),
            v((NZ, LINE, 2, 8, 128), i32), v((NZ, LINE, 2, 8, 128), i32),
            v((NZ, LINE, 5, 8, 128), i32), v((NZ, LINE, 5, 8, 128), i32),
            v(tiles, i32), v(tiles, i32),
            v((cap, 16, 256), bf16), v((PLACES, 2, 8, 128), i32), v((NZ, LINE, 8, 128), i32),
            v((2, 8, 128), f32), v((17, 8, 128), f32), v((3, 8, 128), f32),
            dma((4,)), dma((2,)), dma, dma((NZ,)), dma((NZ,)), dma, dma, dma((NZ,)), dma((NZ,)),
            dma, dma, dma((NZ,)), dma((NZ,)), dma, dma((NZ,)), dma((NZ,)), dma((3,)), dma((3,)),
        ],
        compiler_params=pltpu.CompilerParams(
            collective_id=cid, has_side_effects=True, vmem_limit_bytes=56 * 2**20
        ),
        cost_estimate=pl.CostEstimate(flops=4 * 10**9, bytes_accessed=14 * 10**6, transcendentals=0),
    )(owner, slot, grads.reshape(FLAT), second_moment.reshape(FLAT), left.reshape(fac), right.reshape(fac))


def apply(table, coded, total, new, momentum, cap):
    f32 = jnp.float32
    hbm, vm, sm = spaces()
    dma = pltpu.SemaphoreType.DMA
    out = jax.ShapeDtypeStruct(FLAT, f32)
    return pl.pallas_call(
        functools.partial(finish, cap),
        out_shape=(out, out),
        in_specs=[sm, vm, vm, hbm, hbm],
        out_specs=(hbm, hbm),
        scratch_shapes=[pltpu.VMEM(FLAT, f32), pltpu.VMEM(FLAT, f32), dma((5,)), dma((5,))],
        compiler_params=pltpu.CompilerParams(vmem_limit_bytes=56 * 2**20),
        cost_estimate=pl.CostEstimate(flops=10**6, bytes_accessed=8 * 10**6, transcendentals=0),
    )(table, coded, total, new, momentum.reshape(FLAT))


def general(grads, second_moment, momentum, left, right, owners, slots):
    two, rowblk, rows, width = grads.shape
    colblk = width // B
    g = grads.astype(jnp.float32)
    moment_new = 0.9 * second_moment + 0.1 * g * g
    adam = g / (jnp.sqrt(moment_new) + 1e-08)
    devices = NX * NZ * NC
    pieces = grads.reshape(two, rowblk, rows, colblk, B).transpose(0, 1, 3, 2, 4).reshape(NBLK, rows, B)
    target = slots * devices + owners
    match = target[None, :] == jnp.arange(SLOTS * devices, dtype=jnp.int32)[:, None]
    block_at = jnp.sum(jnp.where(match, jnp.arange(NBLK, dtype=jnp.int32)[None, :], 0), axis=1)
    filled = jnp.any(match, axis=1)
    sent = jnp.where(filled[:, None, None], pieces[block_at], jnp.zeros((), grads.dtype))
    got = lax.all_to_all(sent.reshape(SLOTS, devices, rows, B), "fsdp", split_axis=1, concat_axis=1, tiled=True)
    tile = got.reshape(SLOTS, B, B).astype(jnp.float32)
    full = lax.Precision.HIGHEST
    inner = jnp.einsum("sij,sjk->sik", tile, right[0, 0], precision=full)
    owned = jnp.einsum("sij,sjk->sik", left[0, 0], inner, precision=full)
    back = lax.all_to_all(owned.reshape(SLOTS, devices, rows, B), "fsdp", split_axis=1, concat_axis=1, tiled=True)
    flat = back.reshape(SLOTS * devices, rows, B)[target]
    direction = flat.reshape(two, rowblk, colblk, rows, B).transpose(0, 1, 3, 2, 4).reshape(grads.shape)
    both = jnp.stack([jnp.sum(adam * adam, axis=(1, 2, 3)), jnp.sum(direction * direction, axis=(1, 2, 3))])
    both = lax.psum(both, ("fsdp", "rep"))
    scale = jnp.sqrt(both[0]) / (jnp.sqrt(both[1]) + 1e-06)
    return moment_new.reshape(FLAT), (0.9 * momentum + scale[:, None, None, None] * direction).reshape(FLAT)


def shards(grads, second_moment, momentum, left, right, owner, slot):
    new, coded, total, table = fused(grads, second_moment, left, right, owner, slot, CAP, 0)

    def fast():
        return apply(table, coded, total, new, momentum, CAP)

    def slow():
        return general(grads, second_moment, momentum, left, right, owner[0], slot[0])

    if CAP == PLACES:
        new, mom = fast()
    else:
        new, mom = lax.cond(total[4, 0] > 0.0, slow, fast)
    return new.reshape(second_moment.shape), mom.reshape(momentum.shape)


def solution(mesh):
    in_specs = (
        P(None, None, "fsdp", "rep"),
        P(None, None, "fsdp", "rep"),
        P(None, None, "fsdp", "rep"),
        P("rep", "fsdp", None, None, None),
        P("rep", "fsdp", None, None, None),
        P("rep", None),
        P("rep", None),
    )
    out_specs = (P(None, None, "fsdp", "rep"), P(None, None, "fsdp", "rep"))
    return jax.shard_map(shards, mesh=mesh, in_specs=in_specs, out_specs=out_specs, check_vma=False)
```

```python
import functools

import jax
import jax.numpy as jnp
from jax import lax
from jax.experimental import pallas as pl
from jax.experimental.pallas import tpu as pltpu
from jax.sharding import PartitionSpec as P

MESH = pl.DeviceIdType.MESH
NX, NZ, NC, NREP = 4, 8, 2, 4
LINE = NX * NC
SLOTS = 3
B = 512
NBLK = 96
PLACES = LINE * SLOTS
CAP = 19
LAG = 3
FIRST = 1
HOP1, HOP2 = 2, 5
FLAT = (32, 8, 1536)
T_DEAL, T_COLLECT, T_MINE, T_FIN = 8, 9, 10, 11
STEPS = 16.0


def offset_of(k):
    return jnp.where(k % 2 == 1, (k + 1) // 2, (NZ - k // 2) % NZ)


def within(i, n):
    return jnp.minimum(jnp.maximum(i, 0), n - 1)


def build_tables(owner, slot, x, z, c, cap):
    i32, f32 = jnp.int32, jnp.float32
    sq = (NBLK, NBLK)
    eye = lax.broadcasted_iota(i32, sq, 0) == lax.broadcasted_iota(i32, sq, 1)

    def column(v):
        wide = jnp.broadcast_to(v.astype(f32), sq)
        return jnp.sum(jnp.where(eye, wide, 0.0), axis=1, keepdims=True)

    line = (owner >> 1) & (NZ - 1)
    ox, oc = owner >> 4, owner & 1
    place = (ox * NC + oc) * SLOTS + slot
    linef, placef = line.astype(f32), place.astype(f32)
    line_col, place_col = column(line), column(place)
    before = (jnp.broadcast_to(line_col, sq) == jnp.broadcast_to(linef, sq)) & (
        jnp.broadcast_to(place_col, sq) < jnp.broadcast_to(placef, sq))
    rank = jnp.sum(jnp.where(before, 1.0, 0.0), axis=0, keepdims=True)
    rank_col = column(rank)
    code_col = column((((x - ox) & (NX - 1)) * NC + ((oc + c) & 1)) * SLOTS + slot)
    block_col = lax.broadcasted_iota(i32, (NBLK, 128), 0).astype(f32)
    lane = lax.broadcasted_iota(i32, (NBLK, 128), 1)
    wide = (NBLK, 128)
    line_w, place_w, rank_w, code_w = (jnp.broadcast_to(v, wide) for v in (line_col, place_col, rank_col, code_col))
    lanef = lane.astype(f32)

    def pick(match, value):
        return jnp.sum(jnp.where(match, value, 0.0), axis=0, keepdims=True)

    at_pos = rank_w == lanef
    rows = [jnp.minimum(pick(at_pos & (line_w == ((z + d) & (NZ - 1)).astype(f32)), block_col), NBLK - 1.0) for d in range(NZ)]
    here = line_w == z.astype(f32)
    j = (lane * 11) >> 5
    s = lane - j * SLOTS
    dealt = ((((x + (j >> 1)) & (NX - 1)) * NC + ((c + j) & 1)) * SLOTS + s).astype(f32)
    rows.append(jnp.minimum(pick(here & (place_w == dealt), rank_w), cap - 1.0))
    rows.append(jnp.minimum(pick(here & at_pos, code_w), PLACES - 1.0))
    mine = ((x * NC + c) * SLOTS + lane).astype(f32)
    rows.append(pick(here & (place_w == mine), jnp.where(block_col >= NBLK // 2, 2.0, 1.0)))
    finals = [(z - line) & (NZ - 1), jnp.minimum(rank, cap - 1.0).astype(i32), place]
    top = jnp.max(rank, axis=1, keepdims=True)
    return [r.astype(i32) for r in rows], finals, top


def kernel(cap, owner_ref, slot_ref, g_ref, sm_hbm, left_hbm, right_hbm,
           mn_hbm, zr_hbm, stat_ref, tabv, flag_ref,
           tab, gp, sm, mn, lf, rf, lhi, llo, rhi, rlo, thi, tlo, pbuf,
           zout, zin, xout, xin, xrout, xrin, zrout, zrin, zst, xst, nrm, nin, tot,
           lsem, osem, zs, zr, xs, xr, xrs, xrr, zrs, zrr, ns, nr):
    f = lax.axis_index("fsdp")
    r = lax.axis_index("rep")
    x, z, c = f // (NZ * NC), (f // NC) % NZ, f % NC
    f32 = jnp.float32

    def zdev(d):
        return (x * (NZ * NC) + lax.rem(z + d, NZ) * NC + c, r)

    def xdev(j):
        return (lax.rem(x + j // NC, NX) * (NZ * NC) + z * NC + lax.rem(c + j % NC, NC), r)

    def rdev(i):
        return (f, lax.rem(r + i, NREP))

    peers = [zdev(d) for d in range(1, NZ)] + [xdev(j) for j in range(1, LINE)] + [rdev(i) for i in range(1, NREP)]
    bar = pltpu.get_barrier_semaphore()
    for dev in peers:
        pl.semaphore_signal(bar, 1, device_id=dev, device_id_type=MESH)

    loads = [
        pltpu.make_async_copy(right_hbm, rf, lsem.at[0]),
        pltpu.make_async_copy(sm_hbm, sm, lsem.at[1]),
        pltpu.make_async_copy(left_hbm, lf, lsem.at[2]),
    ]
    for cp in loads:
        cp.start()

    rows, finals, top = build_tables(owner_ref[...], slot_ref[...], x, z, c, cap)
    for i, v in enumerate(rows):
        tabv[pl.ds(i, 1), :] = v
    for i, v in enumerate(finals):
        tabv[pl.ds(T_FIN + i, 1), :] = jnp.zeros((1, 128), jnp.int32)
        tabv[pl.ds(T_FIN + i, 1), pl.ds(0, NBLK)] = v
    tabv[pl.ds(T_FIN + 3, 2), :] = jnp.zeros((2, 128), jnp.int32)
    over = jnp.where(top >= cap, 1.0, 0.0)
    tcopy = pltpu.make_async_copy(tabv, tab, lsem.at[3])
    tcopy.start()

    def repack(i, carry):
        row = g_ref[i].astype(f32)
        for q in range(3):
            a = row[:, q * B:q * B + B // 2]
            b = row[:, q * B + B // 2:(q + 1) * B]
            gp[i * 3 + q] = jnp.concatenate([a, b], axis=0).astype(jnp.bfloat16)
        return carry

    lax.fori_loop(0, 32, repack, 0)
    tcopy.wait()

    def fill(d, dst, slot):
        def one(p, carry):
            dst[slot, p] = gp[within(tab[d, p], NBLK)]
            return carry
        lax.fori_loop(0, cap, one, 0, unroll=4)

    def zsend(k, carry):
        d = offset_of(k)
        fill(d, zout, d)

        @pl.when(k == 1)
        def _():
            pl.semaphore_wait(bar, len(peers))

        pltpu.make_async_remote_copy(src_ref=zout.at[d], dst_ref=zin.at[d], send_sem=zs, recv_sem=zr.at[d],
                                     device_id=zdev(d), device_id_type=MESH).start()
        return carry

    lax.fori_loop(1, NZ, zsend, 0)
    fill(0, zin, 0)

    loads[1].wait()

    def adam_m(m):
        def one(k, acc):
            i = m * 16 + k
            g = g_ref[i].astype(f32)
            new = 0.9 * sm[i] + 0.1 * g * g
            mn[i] = new
            a = g / (jnp.sqrt(new) + 1e-8)
            a = a * a
            for q in range(12):
                acc = acc + a[:, q * 128:(q + 1) * 128]
            return acc
        return lax.fori_loop(0, 16, one, jnp.zeros((8, 128), f32))

    adam0 = adam_m(0)
    adam1 = adam_m(1)
    mn_out = pltpu.make_async_copy(mn, mn_hbm, osem.at[0])
    mn_out.start()

    def split(src, hi, lo):
        def one(i, carry):
            for s in range(SLOTS):
                v = src[s, i // NZ, i % NZ]
                h = v.astype(jnp.bfloat16)
                hi[s, i // NZ, i % NZ] = h
                lo[s, i // NZ, i % NZ] = (v - h.astype(f32)).astype(jnp.bfloat16)
            return carry
        lax.fori_loop(0, NX * NZ, one, 0)

    loads[0].wait()
    split(rf, rhi, rlo)
    loads[2].wait()
    split(lf, lhi, llo)

    def whole(ref, s):
        return ref[s].reshape(B, B)

    def xsend(d):
        zst[...] = zin[d]
        for j in range(LINE):
            for s in range(SLOTS):
                piece = zst[within(tab[T_DEAL, j * SLOTS + s], cap)]
                if j:
                    xout[d, j, s] = piece
                else:
                    xin[d, j, s] = piece
            if j:
                pltpu.make_async_remote_copy(src_ref=xout.at[d, j], dst_ref=xin.at[d, j], send_sem=xs,
                                             recv_sem=xr.at[d], device_id=xdev(j), device_id_type=MESH).start()

    def tchunk(d):
        pltpu.make_async_copy(xin.at[d, pl.ds(1, LINE - 1)], xin.at[d, pl.ds(1, LINE - 1)], xr.at[d]).wait()
        zsrc = lax.rem(z - d + NZ, NZ)
        for s in range(SLOTS):
            rows = []
            for dx in range(NX):
                p0 = xin[d, dx * NC + c, s].astype(f32)
                p1 = xin[d, dx * NC + (1 - c), s].astype(f32)
                lft = jnp.concatenate([p0[:8], p1[:8]], axis=0)
                rgt = jnp.concatenate([p0[8:], p1[8:]], axis=0)
                rows.append(jnp.concatenate([lft, rgt], axis=1).astype(jnp.bfloat16))
            a = jnp.concatenate(rows, axis=0)
            t = jnp.dot(a, whole(rhi, s), preferred_element_type=f32) + jnp.dot(a, whole(rlo, s), preferred_element_type=f32)
            h = t.astype(jnp.bfloat16)
            lo = (t - h.astype(f32)).astype(jnp.bfloat16)
            for dx in range(NX):
                xsrc = lax.rem(x - dx + NX, NX)
                thi[s, xsrc, zsrc] = h[dx * 16:(dx + 1) * 16]
                tlo[s, xsrc, zsrc] = lo[dx * 16:(dx + 1) * 16]

    xsend(0)

    def forward(k, carry):
        d = offset_of(k)
        pltpu.make_async_copy(zin.at[d], zin.at[d], zr.at[d]).wait()
        xsend(d)

        @pl.when(k >= LAG)
        def _():
            tchunk(offset_of(k - LAG))
        return carry

    lax.fori_loop(1, NZ, forward, 0)
    lax.fori_loop(NZ - LAG, NZ, lambda k, carry: (tchunk(offset_of(k)), carry)[1], 0)

    lane = lax.broadcasted_iota(jnp.int32, (8, 128), 1)
    row = lax.broadcasted_iota(jnp.int32, (8, 128), 0)
    base = (x * NC + c) * SLOTS
    nrm[...] = jnp.zeros_like(nrm)

    def product(first, count):
        for s in range(SLOTS):
            hs, ls = [], []
            for i in range(count):
                zz = lax.rem(z + offset_of(NZ - 1 - (first + i)), NZ)
                hs.append(lhi[s, :, zz].reshape(64, B))
                ls.append(llo[s, :, zz].reshape(64, B))
            h = jnp.concatenate(hs, axis=0)
            lo = jnp.concatenate(ls, axis=0)
            p = jnp.dot(h, whole(thi, s), preferred_element_type=f32)
            p = p + jnp.dot(h, whole(tlo, s), preferred_element_type=f32)
            p = p + jnp.dot(lo, whole(thi, s), preferred_element_type=f32)
            pbuf[s, pl.ds(first * 64, count * 64), :] = p

    def tally(i, carry):
        for s in range(SLOTS):
            acc = jnp.zeros((8, 128), f32)
            for u in range(8):
                v = pbuf[s, pl.ds(pl.multiple_of(i * 64 + u * 8, 8), 8), :]
                sq = v * v
                acc = acc + ((sq[:, :128] + sq[:, 128:256]) + (sq[:, 256:384] + sq[:, 384:]))
            which = tab[T_MINE, s]
            nrm[0] += jnp.where(which == 1, acc, 0.0)
            nrm[1] += jnp.where(which == 2, acc, 0.0)
        return carry

    def encode(i, carry):
        d = offset_of(NZ - 1 - i)
        for xd in range(NX):
            for cd in range(NC):
                j = lax.rem(xd - x + NX, NX) * NC + lax.rem(cd + c, NC)
                lev = jnp.zeros((8, 128), jnp.int32)
                at = pl.multiple_of(i * 64 + (xd * NC + cd) * 8, 8)
                for s in range(SLOTS):
                    v = pbuf[s, pl.ds(at, 8), :]
                    top = jnp.maximum(jnp.max(jnp.abs(v), axis=1, keepdims=True), 1e-30)
                    level = jnp.ceil(jnp.log2(top) * STEPS) + 1.0
                    q = jnp.round(v * (jnp.exp2(level * (-1.0 / STEPS)) * 32767.0)).astype(jnp.int32)
                    packed = (q[:, :256] << 16) | (q[:, 256:] & 0xFFFF)
                    xrout[d, j, 2 * s] = packed[:, :128]
                    xrout[d, j, 2 * s + 1] = packed[:, 128:]
                    lev = jnp.where(lane == base + s, level.astype(jnp.int32), lev)
                xrout[d, j, 2 * SLOTS] = lev
        xrin[d, 0] = xrout[d, 0]
        for j in range(1, LINE):
            pltpu.make_async_remote_copy(src_ref=xrout.at[d, j], dst_ref=xrin.at[d, j], send_sem=xrs,
                                         recv_sem=xrr.at[d], device_id=xdev(j), device_id_type=MESH).start()
        return carry

    def relay(k):
        d = offset_of(NZ - 1 - k)
        pltpu.make_async_copy(xrin.at[d, pl.ds(1, LINE - 1)], xrin.at[d, pl.ds(1, LINE - 1)], xrr.at[d]).wait()

        def put(dst):
            for j in range(LINE):
                for s in range(SLOTS):
                    xst[j * SLOTS + s, 0] = xrin[d, j, 2 * s]
                    xst[j * SLOTS + s, 1] = xrin[d, j, 2 * s + 1]

            def one(p, carry):
                code = within(tab[T_COLLECT, p], PLACES)
                dst[d, 2 * p] = xst[code, 0]
                dst[d, 2 * p + 1] = xst[code, 1]
                return carry
            lax.fori_loop(0, cap, one, 0, unroll=4)
            lev = xrin[d, 0, 2 * SLOTS]
            for j in range(1, LINE):
                lev = lev + xrin[d, j, 2 * SLOTS]
            dst[d, 2 * cap] = lev
        return d, put

    def relay_out(k, carry):
        d, put = relay(k)
        put(zrout)
        pltpu.make_async_remote_copy(src_ref=zrout.at[d], dst_ref=zrin.at[d], send_sem=zrs, recv_sem=zrr.at[d],
                                     device_id=zdev(d), device_id_type=MESH).start()
        return carry

    def pack_row(i, v):
        return jnp.where(row == i, jnp.sum(v, axis=0, keepdims=True), 0.0)

    def share(stage, devs, base_at):
        for i, dev in enumerate(devs):
            pltpu.make_async_remote_copy(src_ref=tot.at[stage], dst_ref=nin.at[base_at + i], send_sem=ns.at[stage],
                                         recv_sem=nr.at[stage], device_id=dev, device_id_type=MESH).start()

    def gather(stage, count, base_at):
        view = nin.at[pl.ds(base_at, count)]
        pltpu.make_async_copy(view, view, nr.at[stage]).wait()
        acc = tot[stage]
        for i in range(count):
            acc = acc + nin[base_at + i]
        return acc

    product(0, FIRST)
    lax.fori_loop(0, FIRST, encode, 0)
    product(FIRST, NZ - FIRST)
    lax.fori_loop(0, NZ, tally, 0)
    local = pack_row(0, adam0) + pack_row(1, adam1) + pack_row(2, nrm[0]) + pack_row(3, nrm[1])
    tot[0] = local + jnp.where(row == 4, over, 0.0)

    share(0, [xdev(j) for j in range(1, LINE)], 0)
    lax.fori_loop(FIRST, NZ, encode, 0)
    lax.fori_loop(0, HOP1, relay_out, 0)
    tot[1] = gather(0, LINE - 1, 0)
    share(1, [zdev(d) for d in range(1, NZ)], 7)
    lax.fori_loop(HOP1, HOP2, relay_out, 0)
    tot[2] = gather(1, NZ - 1, 7)
    share(2, [rdev(i) for i in range(1, NREP)], 14)
    lax.fori_loop(HOP2, NZ - 1, relay_out, 0)
    d, put = relay(NZ - 1)
    put(zrin)
    total = gather(2, NREP - 1, 14)
    stat_ref[...] = total
    flag_ref[0] = (stat_ref[4, 0] > 0.0).astype(jnp.int32)

    def ship(d):
        return pltpu.make_async_copy(zrin.at[d], zr_hbm.at[d], osem.at[1])

    def landed(k, carry):
        d = offset_of(NZ - k)
        pltpu.make_async_copy(zrin.at[d], zrin.at[d], zrr.at[d]).wait()
        ship(d).start()
        return carry

    ship(0).start()
    lax.fori_loop(1, NZ, landed, 0)

    def sent(ref, sem):
        pltpu.make_async_copy(ref, ref, sem).wait()

    sent(zout.at[pl.ds(1, NZ - 1)], zs)
    sent(xout.at[:, pl.ds(1, LINE - 1)], xs)
    sent(xrout.at[:, pl.ds(1, LINE - 1)], xrs)
    sent(zrout.at[pl.ds(1, NZ - 1)], zrs)
    sent(nin.at[pl.ds(0, 7)], ns.at[0])
    sent(nin.at[pl.ds(7, 7)], ns.at[1])
    sent(nin.at[pl.ds(14, 3)], ns.at[2])
    mn_out.wait()
    pltpu.make_async_copy(zrin, zr_hbm, osem.at[1]).wait()


def finish(cap, tab, coded_hbm, total, mn_hbm, mom_hbm, mn_out, out_hbm, zin, mom, mn, osem, lsem):
    parts = 4
    per = 32 // parts
    coded = pltpu.make_async_copy(coded_hbm, zin, lsem.at[parts + 1])
    coded.start()
    loads = []
    for i in range(parts):
        view = pl.ds(i * per, per)
        loads.append(pltpu.make_async_copy(mom_hbm.at[view], mom.at[view], lsem.at[i]))
        loads[-1].start()
    fetch = pltpu.make_async_copy(mn_hbm, mn, lsem.at[parts])
    fetch.start()
    copy = pltpu.make_async_copy(mn, mn_out, osem.at[parts])
    sums = jnp.sum(total[...], axis=1, keepdims=True)
    scale = jnp.sqrt(sums[0:2]) / (jnp.sqrt(sums[2:4]) + 1e-6) * (1.0 / 32767.0)
    lane = lax.broadcasted_iota(jnp.int32, (8, 128), 1)
    outs = []
    coded.wait()
    for n in range(parts):
        m = n * 2 // parts
        factor = scale[m:m + 1]

        def one(k, carry):
            i = n * per + k
            for q in range(3):
                b = i * 3 + q
                d, p, e = tab[T_FIN, b], tab[T_FIN + 1, b], tab[T_FIN + 2, b]
                lev = jnp.sum(jnp.where(lane == e, zin[d, 2 * cap], 0).astype(jnp.float32), axis=1, keepdims=True)
                mul = jnp.exp2(lev * (1.0 / STEPS)) * factor
                for h in range(2):
                    w = zin[d, 2 * p + h]
                    for u, v in ((0, w >> 16), (1, (w << 16) >> 16)):
                        cols = pl.ds(q * B + u * 256 + h * 128, 128)
                        mom[i, :, cols] = 0.9 * mom[i, :, cols] + v.astype(jnp.float32) * mul
            return carry

        loads[n].wait()
        lax.fori_loop(0, per, one, 0, unroll=4)
        view = pl.ds(n * per, per)
        outs.append(pltpu.make_async_copy(mom.at[view], out_hbm.at[view], osem.at[n]))
        outs[-1].start()
        if n == 0:
            fetch.wait()
            copy.start()
    copy.wait()
    for cp in outs:
        cp.wait()


def spaces():
    return (pl.BlockSpec(memory_space=s) for s in (pl.ANY, pltpu.VMEM, pltpu.SMEM))


def fused(grads, second_moment, left, right, owner, slot, cap, cid):
    bf16, f32, i32 = jnp.bfloat16, jnp.float32, jnp.int32
    fac = (SLOTS, NX, NZ, 16, B)
    v, dma = pltpu.VMEM, pltpu.SemaphoreType.DMA
    hbm, vm, sm = spaces()
    tiles = (NZ, 2 * cap + 1, 8, 128)
    return pl.pallas_call(
        functools.partial(kernel, cap),
        out_shape=(
            jax.ShapeDtypeStruct(FLAT, f32),
            jax.ShapeDtypeStruct(tiles, i32),
            jax.ShapeDtypeStruct((8, 128), f32),
            jax.ShapeDtypeStruct((16, 128), i32),
            jax.ShapeDtypeStruct((1,), i32),
        ),
        in_specs=[vm, vm, vm, hbm, hbm, hbm],
        out_specs=(hbm, hbm, vm, vm, sm),
        scratch_shapes=[
            pltpu.SMEM((16, 128), i32),
            v((NBLK, 16, 256), bf16), v(FLAT, f32), v(FLAT, f32),
            v(fac, f32), v(fac, f32), v(fac, bf16), v(fac, bf16), v(fac, bf16), v(fac, bf16),
            v(fac, bf16), v(fac, bf16), v((SLOTS, B, B), f32),
            v((NZ, cap, 16, 256), bf16), v((NZ, cap, 16, 256), bf16),
            v((NZ, LINE, SLOTS, 16, 256), bf16), v((NZ, LINE, SLOTS, 16, 256), bf16),
            v((NZ, LINE, 2 * SLOTS + 1, 8, 128), i32), v((NZ, LINE, 2 * SLOTS + 1, 8, 128), i32),
            v(tiles, i32), v(tiles, i32),
            v((cap, 16, 256), bf16), v((PLACES, 2, 8, 128), i32),
            v((2, 8, 128), f32), v((17, 8, 128), f32), v((3, 8, 128), f32),
            dma((4,)), dma((2,)), dma, dma((NZ,)), dma, dma((NZ,)), dma, dma((NZ,)), dma, dma((NZ,)),
            dma((3,)), dma((3,)),
        ],
        compiler_params=pltpu.CompilerParams(
            collective_id=cid, has_side_effects=True, vmem_limit_bytes=56 * 2**20
        ),
        cost_estimate=pl.CostEstimate(flops=4 * 10**9, bytes_accessed=14 * 10**6, transcendentals=0),
    )(owner, slot, grads.reshape(FLAT), second_moment.reshape(FLAT), left.reshape(fac), right.reshape(fac))


def apply(table, coded, total, new, momentum, cap):
    f32 = jnp.float32
    hbm, vm, sm = spaces()
    dma = pltpu.SemaphoreType.DMA
    out = jax.ShapeDtypeStruct(FLAT, f32)
    return pl.pallas_call(
        functools.partial(finish, cap),
        out_shape=(out, out),
        in_specs=[sm, hbm, vm, hbm, hbm],
        out_specs=(hbm, hbm),
        scratch_shapes=[pltpu.VMEM(coded.shape, coded.dtype), pltpu.VMEM(FLAT, f32), pltpu.VMEM(FLAT, f32), dma((5,)), dma((6,))],
        compiler_params=pltpu.CompilerParams(vmem_limit_bytes=56 * 2**20),
        cost_estimate=pl.CostEstimate(flops=10**6, bytes_accessed=8 * 10**6, transcendentals=0),
    )(table, coded, total, new, momentum.reshape(FLAT))


def general(grads, second_moment, momentum, left, right, owners, slots):
    two, rowblk, rows, width = grads.shape
    colblk = width // B
    g = grads.astype(jnp.float32)
    moment_new = 0.9 * second_moment + 0.1 * g * g
    adam = g / (jnp.sqrt(moment_new) + 1e-08)
    devices = NX * NZ * NC
    pieces = grads.reshape(two, rowblk, rows, colblk, B).transpose(0, 1, 3, 2, 4).reshape(NBLK, rows, B)
    target = slots * devices + owners
    match = target[None, :] == jnp.arange(SLOTS * devices, dtype=jnp.int32)[:, None]
    block_at = jnp.sum(jnp.where(match, jnp.arange(NBLK, dtype=jnp.int32)[None, :], 0), axis=1)
    filled = jnp.any(match, axis=1)
    sent = jnp.where(filled[:, None, None], pieces[block_at], jnp.zeros((), grads.dtype))
    got = lax.all_to_all(sent.reshape(SLOTS, devices, rows, B), "fsdp", split_axis=1, concat_axis=1, tiled=True)
    tile = got.reshape(SLOTS, B, B).astype(jnp.float32)
    full = lax.Precision.HIGHEST
    inner = jnp.einsum("sij,sjk->sik", tile, right[0, 0], precision=full)
    owned = jnp.einsum("sij,sjk->sik", left[0, 0], inner, precision=full)
    back = lax.all_to_all(owned.reshape(SLOTS, devices, rows, B), "fsdp", split_axis=1, concat_axis=1, tiled=True)
    flat = back.reshape(SLOTS * devices, rows, B)[target]
    direction = flat.reshape(two, rowblk, colblk, rows, B).transpose(0, 1, 3, 2, 4).reshape(grads.shape)
    both = jnp.stack([jnp.sum(adam * adam, axis=(1, 2, 3)), jnp.sum(direction * direction, axis=(1, 2, 3))])
    both = lax.psum(both, ("fsdp", "rep"))
    scale = jnp.sqrt(both[0]) / (jnp.sqrt(both[1]) + 1e-06)
    return moment_new.reshape(FLAT), (0.9 * momentum + scale[:, None, None, None] * direction).reshape(FLAT)


def shards(grads, second_moment, momentum, left, right, owner, slot):
    new, coded, total, table, flag = fused(grads, second_moment, left, right, owner, slot, CAP, 0)

    def fast():
        return apply(table, coded, total, new, momentum, CAP)

    def slow():
        return general(grads, second_moment, momentum, left, right, owner[0], slot[0])

    if CAP == PLACES:
        new, mom = fast()
    else:
        new, mom = lax.cond(flag[0] > 0, slow, fast)
    return new.reshape(second_moment.shape), mom.reshape(momentum.shape)


def solution(mesh):
    in_specs = (
        P(None, None, "fsdp", "rep"),
        P(None, None, "fsdp", "rep"),
        P(None, None, "fsdp", "rep"),
        P("rep", "fsdp", None, None, None),
        P("rep", "fsdp", None, None, None),
        P("rep", None),
        P("rep", None),
    )
    out_specs = (P(None, None, "fsdp", "rep"), P(None, None, "fsdp", "rep"))
    return jax.shard_map(shards, mesh=mesh, in_specs=in_specs, out_specs=out_specs, check_vma=False)
```

```python
import functools

import jax
import jax.numpy as jnp
from jax import lax
from jax.experimental import pallas as pl
from jax.experimental.pallas import tpu as pltpu
from jax.sharding import PartitionSpec as P

MESH = pl.DeviceIdType.MESH
NX, NZ, NC, NREP = 4, 8, 2, 4
LINE = NX * NC
SLOTS = 3
B = 512
NBLK = 96
PLACES = LINE * SLOTS
CAP = 19
LAG_A = 3
LAG_B = 4
FIRST = 1
HOP1, HOP2 = 2, 5
EARLY = 5
FLAT = (32, 8, 1536)
T_DEAL, T_COLLECT, T_MINE, T_FIN = 8, 9, 10, 11
STEPS = 16.0


def offset_of(k):
    return jnp.where(k % 2 == 1, (k + 1) // 2, (NZ - k // 2) % NZ)


def within(i, n):
    return jnp.minimum(jnp.maximum(i, 0), n - 1)


def build_tables(owner, slot, x, z, c, cap):
    i32, f32 = jnp.int32, jnp.float32
    sq = (NBLK, NBLK)
    eye = lax.broadcasted_iota(i32, sq, 0) == lax.broadcasted_iota(i32, sq, 1)

    def column(v):
        wide = jnp.broadcast_to(v.astype(f32), sq)
        return jnp.sum(jnp.where(eye, wide, 0.0), axis=1, keepdims=True)

    line = (owner >> 1) & (NZ - 1)
    ox, oc = owner >> 4, owner & 1
    place = slot * LINE + ox * NC + oc
    linef, placef = line.astype(f32), place.astype(f32)
    line_col, place_col = column(line), column(place)
    before = (jnp.broadcast_to(line_col, sq) == jnp.broadcast_to(linef, sq)) & (
        jnp.broadcast_to(place_col, sq) < jnp.broadcast_to(placef, sq))
    rank = jnp.sum(jnp.where(before, 1.0, 0.0), axis=0, keepdims=True)
    rank_col = column(rank)
    firsts = (jnp.broadcast_to(line_col, sq) == jnp.broadcast_to(linef, sq)) & (
        jnp.broadcast_to(place_col, sq) < float(LINE))
    spare = jnp.maximum(EARLY - jnp.sum(jnp.where(firsts, 1.0, 0.0), axis=0, keepdims=True), 0.0)
    seat = jnp.where((slot == 0) & (rank < float(EARLY)), rank, rank + spare)
    seat_col = column(seat)
    code_col = column(slot * LINE + ((x - ox) & (NX - 1)) * NC + ((oc + c) & 1))
    block_col = lax.broadcasted_iota(i32, (NBLK, 128), 0).astype(f32)
    lane = lax.broadcasted_iota(i32, (NBLK, 128), 1)
    wide = (NBLK, 128)
    line_w, place_w, rank_w, code_w, seat_w = (
        jnp.broadcast_to(v, wide) for v in (line_col, place_col, rank_col, code_col, seat_col))
    lanef = lane.astype(f32)

    def pick(match, value):
        return jnp.sum(jnp.where(match, value, 0.0), axis=0, keepdims=True)

    at_pos = rank_w == lanef
    most = float(NBLK - 1)
    rows = [jnp.minimum(pick(at_pos & (line_w == ((z + d) & (NZ - 1)).astype(f32)), block_col), most) for d in range(NZ)]
    here = line_w == z.astype(f32)
    j = lane & (LINE - 1)
    dealt = ((lane - j) + ((x + (j >> 1)) & (NX - 1)) * NC + ((c + j) & 1)).astype(f32)
    rows.append(jnp.minimum(pick(here & (place_w == dealt), rank_w), cap - 1.0))
    rows.append(jnp.minimum(pick(here & (seat_w == lanef), code_w), PLACES - 1.0))
    mine = (x * NC + c + lane * LINE).astype(f32)
    rows.append(pick(here & (place_w == mine), jnp.where(block_col >= NBLK // 2, 2.0, 1.0)))
    finals = [(z - line) & (NZ - 1), jnp.minimum(seat, cap - 1.0).astype(i32), (ox * NC + oc) * SLOTS + slot]
    top = jnp.max(seat, axis=1, keepdims=True)
    return [r.astype(i32) for r in rows], finals, top


def kernel(cap, owner_ref, slot_ref, g_ref, sm_hbm, left_hbm, right_hbm,
           mn_hbm, zr_hbm, stat_ref, tabv, flag_ref,
           tab, gp, sm, mn, lf, rf, lhi, llo, rhi, rlo, thi, tlo, pbuf,
           zout, zin, xout_a, xin_a, xout_b, xin_b, xr_a, xi_a, xr_b, xi_b, zrout, zrin, zst, xst, lev0, nrm, nin, tot,
           lsem, osem, zs, zr_a, zr_b, xs_a, xs_b, xw_a, xw_b, xrs_a, xrs_b, xrw_a, xrw_b, zrs, zrw_a, zrw_b, ns, nr):
    f = lax.axis_index("fsdp")
    r = lax.axis_index("rep")
    x, z, c = f // (NZ * NC), (f // NC) % NZ, f % NC
    f32, bf16 = jnp.float32, jnp.bfloat16

    def zdev(d):
        return (x * (NZ * NC) + lax.rem(z + d, NZ) * NC + c, r)

    def xdev(j):
        return (lax.rem(x + j // NC, NX) * (NZ * NC) + z * NC + lax.rem(c + j % NC, NC), r)

    def rdev(i):
        return (f, lax.rem(r + i, NREP))

    def push(src, dst, ssem, rsem, dev):
        pltpu.make_async_remote_copy(src_ref=src, dst_ref=dst, send_sem=ssem, recv_sem=rsem,
                                     device_id=dev, device_id_type=MESH).start()

    def done(ref, sem):
        pltpu.make_async_copy(ref, ref, sem).wait()

    peers = [zdev(d) for d in range(1, NZ)] + [xdev(j) for j in range(1, LINE)] + [rdev(i) for i in range(1, NREP)]
    bar = pltpu.get_barrier_semaphore()
    for dev in peers:
        pl.semaphore_signal(bar, 1, device_id=dev, device_id_type=MESH)

    loads = [
        pltpu.make_async_copy(right_hbm, rf, lsem.at[0]),
        pltpu.make_async_copy(left_hbm, lf, lsem.at[2]),
        pltpu.make_async_copy(sm_hbm, sm, lsem.at[1]),
    ]
    for cp in loads:
        cp.start()

    rows, finals, top = build_tables(owner_ref[...], slot_ref[...], x, z, c, cap)
    for i, v in enumerate(rows):
        tabv[pl.ds(i, 1), :] = v
    for i, v in enumerate(finals):
        tabv[pl.ds(T_FIN + i, 1), :] = jnp.zeros((1, 128), jnp.int32)
        tabv[pl.ds(T_FIN + i, 1), pl.ds(0, NBLK)] = v
    tabv[pl.ds(T_FIN + 3, 2), :] = jnp.zeros((2, 128), jnp.int32)
    over = jnp.where(top >= cap, 1.0, 0.0)
    tcopy = pltpu.make_async_copy(tabv, tab, lsem.at[3])
    tcopy.start()

    def repack(i, carry):
        row = g_ref[i].astype(f32)
        for q in range(3):
            a = row[:, q * B:q * B + B // 2]
            b = row[:, q * B + B // 2:(q + 1) * B]
            gp[i * 3 + q] = jnp.concatenate([a, b], axis=0).astype(bf16)
        return carry

    lax.fori_loop(0, 32, repack, 0)
    tcopy.wait()

    def fill(d, dst, lo, hi):
        for p in range(lo, hi):
            dst[d, p] = gp[within(tab[d, p], NBLK)]

    part_a, part_b = pl.ds(0, LINE), pl.ds(LINE, cap - LINE)

    def zsend_a(k, carry):
        d = offset_of(k)
        fill(d, zout, 0, LINE)

        @pl.when(k == 1)
        def _():
            pl.semaphore_wait(bar, len(peers))

        push(zout.at[d, part_a], zin.at[d, part_a], zs, zr_a.at[d], zdev(d))
        return carry

    def zsend_b(k, carry):
        d = offset_of(k)
        fill(d, zout, LINE, cap)
        push(zout.at[d, part_b], zin.at[d, part_b], zs, zr_b.at[d], zdev(d))
        return carry

    lax.fori_loop(1, NZ, zsend_a, 0)
    lax.fori_loop(1, NZ, zsend_b, 0)
    fill(0, zin, 0, cap)

    def split(src, hi, lo):
        def one(i, carry):
            for s in range(SLOTS):
                v = src[s, i // NZ, i % NZ]
                h = v.astype(bf16)
                hi[s, i // NZ, i % NZ] = h
                lo[s, i // NZ, i % NZ] = (v - h.astype(f32)).astype(bf16)
            return carry
        lax.fori_loop(0, NX * NZ, one, 0)

    loads[0].wait()
    split(rf, rhi, rlo)
    loads[1].wait()
    split(lf, lhi, llo)

    def whole(ref, s):
        return ref[s].reshape(B, B)

    def tiles(d, s, piece):
        zsrc = lax.rem(z - d + NZ, NZ)
        blocks = []
        for dx in range(NX):
            p0 = piece(dx * NC + c).astype(f32)
            p1 = piece(dx * NC + (1 - c)).astype(f32)
            lft = jnp.concatenate([p0[:8], p1[:8]], axis=0)
            rgt = jnp.concatenate([p0[8:], p1[8:]], axis=0)
            blocks.append(jnp.concatenate([lft, rgt], axis=1).astype(bf16))
        a = jnp.concatenate(blocks, axis=0)
        t = jnp.dot(a, whole(rhi, s), preferred_element_type=f32) + jnp.dot(a, whole(rlo, s), preferred_element_type=f32)
        h = t.astype(bf16)
        lo = (t - h.astype(f32)).astype(bf16)
        for dx in range(NX):
            xsrc = lax.rem(x - dx + NX, NX)
            thi[s, xsrc, zsrc] = h[dx * 16:(dx + 1) * 16]
            tlo[s, xsrc, zsrc] = lo[dx * 16:(dx + 1) * 16]

    others = pl.ds(1, LINE - 1)

    def xsend_a(d):
        zst[pl.ds(0, LINE)] = zin[d, pl.ds(0, LINE)]
        for j in range(LINE):
            piece = zst[within(tab[T_DEAL, j], LINE)]
            if j:
                xout_a[d, j] = piece
                push(xout_a.at[d, j], xin_a.at[d, j], xs_a, xw_a.at[d], xdev(j))
            else:
                xin_a[d, 0] = piece

    def tchunk_a(d):
        done(xin_a.at[d, others], xw_a.at[d])
        tiles(d, 0, lambda j: xin_a[d, j])

    def xsend_b(d):
        zst[...] = zin[d]
        for j in range(LINE):
            for s in (1, 2):
                piece = zst[within(tab[T_DEAL, s * LINE + j], cap)]
                if j:
                    xout_b[d, j, s - 1] = piece
                else:
                    xin_b[d, 0, s - 1] = piece
            if j:
                push(xout_b.at[d, j], xin_b.at[d, j], xs_b, xw_b.at[d], xdev(j))

    def tchunk_b(d):
        done(xin_b.at[d, others], xw_b.at[d])
        for s in (1, 2):
            tiles(d, s, lambda j, s=s: xin_b[d, j, s - 1])

    xsend_a(0)

    def forward_a(k, carry):
        d = offset_of(k)
        done(zin.at[d, part_a], zr_a.at[d])
        xsend_a(d)

        @pl.when(k >= LAG_A)
        def _():
            tchunk_a(offset_of(k - LAG_A))
        return carry

    lax.fori_loop(1, NZ, forward_a, 0)
    lax.fori_loop(NZ - LAG_A, NZ, lambda k, carry: (tchunk_a(offset_of(k)), carry)[1], 0)

    lane = lax.broadcasted_iota(jnp.int32, (8, 128), 1)
    row = lax.broadcasted_iota(jnp.int32, (8, 128), 0)
    base = (x * NC + c) * SLOTS
    nrm[...] = jnp.zeros_like(nrm)

    def back_of(i):
        return offset_of(NZ - 1 - i)

    def product(s, first, count):
        hs, ls = [], []
        for i in range(count):
            zz = lax.rem(z + back_of(first + i), NZ)
            hs.append(lhi[s, :, zz].reshape(64, B))
            ls.append(llo[s, :, zz].reshape(64, B))
        h = jnp.concatenate(hs, axis=0)
        lo = jnp.concatenate(ls, axis=0)
        p = jnp.dot(h, whole(thi, s), preferred_element_type=f32)
        p = p + jnp.dot(h, whole(tlo, s), preferred_element_type=f32)
        return p + jnp.dot(lo, whole(thi, s), preferred_element_type=f32)

    def code_rows(v):
        top = jnp.maximum(jnp.max(jnp.abs(v), axis=1, keepdims=True), 1e-30)
        level = jnp.ceil(jnp.log2(top) * STEPS) + 1.0
        q = jnp.round(v * (jnp.exp2(level * (-1.0 / STEPS)) * 32767.0)).astype(jnp.int32)
        packed = (q[:, :256] << 16) | (q[:, 256:] & 0xFFFF)
        sq = v * v
        return packed, level.astype(jnp.int32), (sq[:, :128] + sq[:, 128:256]) + (sq[:, 256:384] + sq[:, 384:])

    def tally(s, v):
        which = tab[T_MINE, s]
        nrm[0] += jnp.where(which == 1, v, 0.0)
        nrm[1] += jnp.where(which == 2, v, 0.0)

    def target(xd, cd):
        return lax.rem(xd - x + NX, NX) * NC + lax.rem(cd + c, NC)

    pbuf[0] = product(0, 0, NZ)

    def code_a(i, carry):
        d = back_of(i)
        total = jnp.zeros((8, 128), f32)
        for xd in range(NX):
            for cd in range(NC):
                j = target(xd, cd)
                v = pbuf[0, pl.ds(pl.multiple_of(i * 64 + (xd * NC + cd) * 8, 8), 8), :]
                packed, level, sq = code_rows(v)
                total = total + sq
                xr_a[d, j, 0] = packed[:, :128]
                xr_a[d, j, 1] = packed[:, 128:]
                lev0[d, j] = jnp.where(lane == base, level, 0)
        tally(0, total)
        xi_a[d, 0] = xr_a[d, 0]
        for j in range(1, LINE):
            push(xr_a.at[d, j], xi_a.at[d, j], xrs_a, xrw_a.at[d], xdev(j))
        return carry

    lax.fori_loop(0, NZ, code_a, 0)

    loads[2].wait()

    def adam_m(m):
        def one(k, acc):
            i = m * 16 + k
            g = g_ref[i].astype(f32)
            new = 0.9 * sm[i] + 0.1 * g * g
            mn[i] = new
            a = g / (jnp.sqrt(new) + 1e-8)
            a = a * a
            for q in range(12):
                acc = acc + a[:, q * 128:(q + 1) * 128]
            return acc
        return lax.fori_loop(0, 16, one, jnp.zeros((8, 128), f32))

    adam0 = adam_m(0)
    adam1 = adam_m(1)
    mn_out = pltpu.make_async_copy(mn, mn_hbm, osem.at[0])
    mn_out.start()

    seats_a, seats_b = pl.ds(0, 2 * EARLY), pl.ds(2 * EARLY, 2 * (cap - EARLY) + 1)

    def stage_a(d):
        for j in range(LINE):
            xst[j] = xi_a[d, j]

    def seat(dst, d, lo, hi):
        for p in range(lo, hi):
            code = within(tab[T_COLLECT, p], PLACES)
            dst[d, 2 * p] = xst[code, 0]
            dst[d, 2 * p + 1] = xst[code, 1]

    def relay_a(i, dst):
        d = back_of(i)
        done(xi_a.at[d, others], xrw_a.at[d])
        stage_a(d)
        seat(dst, d, 0, EARLY)

    def zback_a(i, carry):
        d = back_of(i)
        relay_a(i, zrout)
        push(zrout.at[d, seats_a], zrin.at[d, seats_a], zrs, zrw_a.at[d], zdev(d))
        return carry

    xsend_b(0)

    def forward_b(k, carry):
        d = offset_of(k)
        done(zin.at[d, part_b], zr_b.at[d])
        xsend_b(d)

        @pl.when(k >= LAG_B)
        def _():
            tchunk_b(offset_of(k - LAG_B))
        return carry

    lax.fori_loop(1, NZ, forward_b, 0)
    lax.fori_loop(0, NZ - 1, zback_a, 0)
    lax.fori_loop(NZ - LAG_B, NZ, lambda k, carry: (tchunk_b(offset_of(k)), carry)[1], 0)

    def multiply(first, count):
        for s in (1, 2):
            pbuf[s, pl.ds(first * 64, count * 64), :] = product(s, first, count)

    def sums_b(i, carry):
        for s in (1, 2):
            acc = jnp.zeros((8, 128), f32)
            for u in range(8):
                v = pbuf[s, pl.ds(pl.multiple_of(i * 64 + u * 8, 8), 8), :]
                sq = v * v
                acc = acc + ((sq[:, :128] + sq[:, 128:256]) + (sq[:, 256:384] + sq[:, 384:]))
            tally(s, acc)
        return carry

    def code_b(i, carry):
        d = back_of(i)
        for xd in range(NX):
            for cd in range(NC):
                j = target(xd, cd)
                lev = lev0[d, j]
                at = pl.ds(pl.multiple_of(i * 64 + (xd * NC + cd) * 8, 8), 8)
                for s in (1, 2):
                    packed, level, _ = code_rows(pbuf[s, at, :])
                    xr_b[d, j, 2 * s - 2] = packed[:, :128]
                    xr_b[d, j, 2 * s - 1] = packed[:, 128:]
                    lev = jnp.where(lane == base + s, level, lev)
                xr_b[d, j, 4] = lev
        xi_b[d, 0] = xr_b[d, 0]
        for j in range(1, LINE):
            push(xr_b.at[d, j], xi_b.at[d, j], xrs_b, xrw_b.at[d], xdev(j))
        return carry

    def relay_b(i, dst):
        d = back_of(i)
        done(xi_b.at[d, others], xrw_b.at[d])
        stage_a(d)
        lev = xi_b[d, 0, 4]
        for j in range(LINE):
            xst[LINE + j] = xi_b[d, j, pl.ds(0, 2)]
            xst[2 * LINE + j] = xi_b[d, j, pl.ds(2, 2)]
            if j:
                lev = lev + xi_b[d, j, 4]
        dst[d, 2 * cap] = lev
        seat(dst, d, EARLY, cap)
        return d

    def relay_out(i, carry):
        d = relay_b(i, zrout)
        push(zrout.at[d, seats_b], zrin.at[d, seats_b], zrs, zrw_b.at[d], zdev(d))
        return carry

    def pack_row(i, v):
        return jnp.where(row == i, jnp.sum(v, axis=0, keepdims=True), 0.0)

    def share(stage, devs, base_at):
        for i, dev in enumerate(devs):
            push(tot.at[stage], nin.at[base_at + i], ns.at[stage], nr.at[stage], dev)

    def gather(stage, count, base_at):
        done(nin.at[pl.ds(base_at, count)], nr.at[stage])
        acc = tot[stage]
        for i in range(count):
            acc = acc + nin[base_at + i]
        return acc

    multiply(0, FIRST)
    lax.fori_loop(0, FIRST, code_b, 0)
    multiply(FIRST, NZ - FIRST)
    lax.fori_loop(0, NZ, sums_b, 0)
    local = pack_row(0, adam0) + pack_row(1, adam1) + pack_row(2, nrm[0]) + pack_row(3, nrm[1])
    tot[0] = local + jnp.where(row == 4, over, 0.0)

    share(0, [xdev(j) for j in range(1, LINE)], 0)
    lax.fori_loop(FIRST, NZ, code_b, 0)
    lax.fori_loop(0, HOP1, relay_out, 0)
    tot[1] = gather(0, LINE - 1, 0)
    share(1, [zdev(d) for d in range(1, NZ)], 7)
    lax.fori_loop(HOP1, HOP2, relay_out, 0)
    tot[2] = gather(1, NZ - 1, 7)
    share(2, [rdev(i) for i in range(1, NREP)], 14)
    lax.fori_loop(HOP2, NZ - 1, relay_out, 0)
    relay_a(NZ - 1, zrin)
    relay_b(NZ - 1, zrin)
    total = gather(2, NREP - 1, 14)
    stat_ref[...] = total
    flag_ref[0] = (stat_ref[4, 0] > 0.0).astype(jnp.int32)

    def ship(d):
        return pltpu.make_async_copy(zrin.at[d], zr_hbm.at[d], osem.at[1 + d])

    def landed(k, carry):
        d = offset_of(NZ - k)
        done(zrin.at[d, seats_a], zrw_a.at[d])
        done(zrin.at[d, seats_b], zrw_b.at[d])
        ship(d).start()
        return carry

    ship(0).start()
    lax.fori_loop(1, NZ, landed, 0)

    done(zout.at[pl.ds(1, NZ - 1)], zs)
    done(xout_a.at[:, others], xs_a)
    done(xout_b.at[:, others], xs_b)
    done(xr_a.at[:, others], xrs_a)
    done(xr_b.at[:, others], xrs_b)
    done(zrout.at[pl.ds(1, NZ - 1)], zrs)
    done(nin.at[pl.ds(0, 7)], ns.at[0])
    done(nin.at[pl.ds(7, 7)], ns.at[1])
    done(nin.at[pl.ds(14, 3)], ns.at[2])
    mn_out.wait()
    for d in range(NZ):
        ship(d).wait()


def finish(cap, tab, coded_hbm, total, mn_hbm, mom_hbm, mn_out, out_hbm, zin, mom, mn, osem, lsem):
    parts = 4
    per = 32 // parts
    coded = pltpu.make_async_copy(coded_hbm, zin, lsem.at[parts + 1])
    coded.start()
    loads = []
    for i in range(parts):
        view = pl.ds(i * per, per)
        loads.append(pltpu.make_async_copy(mom_hbm.at[view], mom.at[view], lsem.at[i]))
        loads[-1].start()
    fetch = pltpu.make_async_copy(mn_hbm, mn, lsem.at[parts])
    fetch.start()
    copy = pltpu.make_async_copy(mn, mn_out, osem.at[parts])
    sums = jnp.sum(total[...], axis=1, keepdims=True)
    scale = jnp.sqrt(sums[0:2]) / (jnp.sqrt(sums[2:4]) + 1e-6) * (1.0 / 32767.0)
    lane = lax.broadcasted_iota(jnp.int32, (8, 128), 1)
    outs = []
    coded.wait()
    for n in range(parts):
        m = n * 2 // parts
        factor = scale[m:m + 1]

        def one(k, carry):
            i = n * per + k
            for q in range(3):
                b = i * 3 + q
                d, p, e = tab[T_FIN, b], tab[T_FIN + 1, b], tab[T_FIN + 2, b]
                lev = jnp.sum(jnp.where(lane == e, zin[d, 2 * cap], 0).astype(jnp.float32), axis=1, keepdims=True)
                mul = jnp.exp2(lev * (1.0 / STEPS)) * factor
                for h in range(2):
                    w = zin[d, 2 * p + h]
                    for u, v in ((0, w >> 16), (1, (w << 16) >> 16)):
                        cols = pl.ds(q * B + u * 256 + h * 128, 128)
                        mom[i, :, cols] = 0.9 * mom[i, :, cols] + v.astype(jnp.float32) * mul
            return carry

        loads[n].wait()
        lax.fori_loop(0, per, one, 0, unroll=4)
        view = pl.ds(n * per, per)
        outs.append(pltpu.make_async_copy(mom.at[view], out_hbm.at[view], osem.at[n]))
        outs[-1].start()
        if n == 0:
            fetch.wait()
            copy.start()
    copy.wait()
    for cp in outs:
        cp.wait()


def spaces():
    return (pl.BlockSpec(memory_space=s) for s in (pl.ANY, pltpu.VMEM, pltpu.SMEM))


def fused(grads, second_moment, left, right, owner, slot, cap, cid):
    bf16, f32, i32 = jnp.bfloat16, jnp.float32, jnp.int32
    fac = (SLOTS, NX, NZ, 16, B)
    v, dma = pltpu.VMEM, pltpu.SemaphoreType.DMA
    hbm, vm, sm = spaces()
    tiles = (NZ, 2 * cap + 1, 8, 128)
    return pl.pallas_call(
        functools.partial(kernel, cap),
        out_shape=(
            jax.ShapeDtypeStruct(FLAT, f32),
            jax.ShapeDtypeStruct(tiles, i32),
            jax.ShapeDtypeStruct((8, 128), f32),
            jax.ShapeDtypeStruct((16, 128), i32),
            jax.ShapeDtypeStruct((1,), i32),
        ),
        in_specs=[vm, vm, vm, hbm, hbm, hbm],
        out_specs=(hbm, hbm, vm, vm, sm),
        scratch_shapes=[
            pltpu.SMEM((16, 128), i32),
            v((NBLK, 16, 256), bf16), v(FLAT, f32), v(FLAT, f32),
            v(fac, f32), v(fac, f32), v(fac, bf16), v(fac, bf16), v(fac, bf16), v(fac, bf16),
            v(fac, bf16), v(fac, bf16), v((SLOTS, B, B), f32),
            v((NZ, cap, 16, 256), bf16), v((NZ, cap, 16, 256), bf16),
            v((NZ, LINE, 16, 256), bf16), v((NZ, LINE, 16, 256), bf16),
            v((NZ, LINE, 2, 16, 256), bf16), v((NZ, LINE, 2, 16, 256), bf16),
            v((NZ, LINE, 2, 8, 128), i32), v((NZ, LINE, 2, 8, 128), i32),
            v((NZ, LINE, 5, 8, 128), i32), v((NZ, LINE, 5, 8, 128), i32),
            v(tiles, i32), v(tiles, i32),
            v((cap, 16, 256), bf16), v((PLACES, 2, 8, 128), i32), v((NZ, LINE, 8, 128), i32),
            v((2, 8, 128), f32), v((17, 8, 128), f32), v((3, 8, 128), f32),
            dma((4,)), dma((1 + NZ,)), dma, dma((NZ,)), dma((NZ,)), dma, dma, dma((NZ,)), dma((NZ,)),
            dma, dma, dma((NZ,)), dma((NZ,)), dma, dma((NZ,)), dma((NZ,)), dma((3,)), dma((3,)),
        ],
        compiler_params=pltpu.CompilerParams(
            collective_id=cid, has_side_effects=True, vmem_limit_bytes=56 * 2**20
        ),
        cost_estimate=pl.CostEstimate(flops=4 * 10**9, bytes_accessed=14 * 10**6, transcendentals=0),
    )(owner, slot, grads.reshape(FLAT), second_moment.reshape(FLAT), left.reshape(fac), right.reshape(fac))


def apply(table, coded, total, new, momentum, cap):
    f32 = jnp.float32
    hbm, vm, sm = spaces()
    dma = pltpu.SemaphoreType.DMA
    out = jax.ShapeDtypeStruct(FLAT, f32)
    return pl.pallas_call(
        functools.partial(finish, cap),
        out_shape=(out, out),
        in_specs=[sm, hbm, vm, hbm, hbm],
        out_specs=(hbm, hbm),
        scratch_shapes=[pltpu.VMEM(coded.shape, coded.dtype), pltpu.VMEM(FLAT, f32), pltpu.VMEM(FLAT, f32), dma((5,)), dma((6,))],
        compiler_params=pltpu.CompilerParams(vmem_limit_bytes=56 * 2**20),
        cost_estimate=pl.CostEstimate(flops=10**6, bytes_accessed=8 * 10**6, transcendentals=0),
    )(table, coded, total, new, momentum.reshape(FLAT))


def general(grads, second_moment, momentum, left, right, owners, slots):
    two, rowblk, rows, width = grads.shape
    colblk = width // B
    g = grads.astype(jnp.float32)
    moment_new = 0.9 * second_moment + 0.1 * g * g
    adam = g / (jnp.sqrt(moment_new) + 1e-08)
    devices = NX * NZ * NC
    pieces = grads.reshape(two, rowblk, rows, colblk, B).transpose(0, 1, 3, 2, 4).reshape(NBLK, rows, B)
    target = slots * devices + owners
    match = target[None, :] == jnp.arange(SLOTS * devices, dtype=jnp.int32)[:, None]
    block_at = jnp.sum(jnp.where(match, jnp.arange(NBLK, dtype=jnp.int32)[None, :], 0), axis=1)
    filled = jnp.any(match, axis=1)
    sent = jnp.where(filled[:, None, None], pieces[block_at], jnp.zeros((), grads.dtype))
    got = lax.all_to_all(sent.reshape(SLOTS, devices, rows, B), "fsdp", split_axis=1, concat_axis=1, tiled=True)
    tile = got.reshape(SLOTS, B, B).astype(jnp.float32)
    full = lax.Precision.HIGHEST
    inner = jnp.einsum("sij,sjk->sik", tile, right[0, 0], precision=full)
    owned = jnp.einsum("sij,sjk->sik", left[0, 0], inner, precision=full)
    back = lax.all_to_all(owned.reshape(SLOTS, devices, rows, B), "fsdp", split_axis=1, concat_axis=1, tiled=True)
    flat = back.reshape(SLOTS * devices, rows, B)[target]
    direction = flat.reshape(two, rowblk, colblk, rows, B).transpose(0, 1, 3, 2, 4).reshape(grads.shape)
    both = jnp.stack([jnp.sum(adam * adam, axis=(1, 2, 3)), jnp.sum(direction * direction, axis=(1, 2, 3))])
    both = lax.psum(both, ("fsdp", "rep"))
    scale = jnp.sqrt(both[0]) / (jnp.sqrt(both[1]) + 1e-06)
    return moment_new.reshape(FLAT), (0.9 * momentum + scale[:, None, None, None] * direction).reshape(FLAT)


def shards(grads, second_moment, momentum, left, right, owner, slot):
    new, coded, total, table, flag = fused(grads, second_moment, left, right, owner, slot, CAP, 0)

    def fast():
        return apply(table, coded, total, new, momentum, CAP)

    def slow():
        return general(grads, second_moment, momentum, left, right, owner[0], slot[0])

    if CAP == PLACES:
        new, mom = fast()
    else:
        new, mom = lax.cond(flag[0] > 0, slow, fast)
    return new.reshape(second_moment.shape), mom.reshape(momentum.shape)


def solution(mesh):
    in_specs = (
        P(None, None, "fsdp", "rep"),
        P(None, None, "fsdp", "rep"),
        P(None, None, "fsdp", "rep"),
        P("rep", "fsdp", None, None, None),
        P("rep", "fsdp", None, None, None),
        P("rep", None),
        P("rep", None),
    )
    out_specs = (P(None, None, "fsdp", "rep"), P(None, None, "fsdp", "rep"))
    return jax.shard_map(shards, mesh=mesh, in_specs=in_specs, out_specs=out_specs, check_vma=False)
```
